128 devices in a mesh: band: 16 (over x, z), mesh: 8 (over y, core).
Axes of the slice: x: 4, y: 4, z: 4, core: 2. Of those that a mesh axis runs over, the one named last changes fastest.
Arguments:
- grid_latent: bfloat16 [131072, 512], P(('band', 'mesh')), may hold values from -6 to 6
- mesh_latent: bfloat16 [8192, 512], P(('band', 'mesh')), may hold values from -6 to 6
- w_src_enc: bfloat16 [512, 512], replicated, may hold values from -0.25 to 0.25
- w_dst_enc: bfloat16 [512, 512], replicated, may hold values from -0.25 to 0.25
- w_out_enc: bfloat16 [512, 512], replicated, may hold values from -0.25 to 0.25
- w_src_dec: bfloat16 [512, 512], replicated, may hold values from -0.25 to 0.25
- w_dst_dec: bfloat16 [512, 512], replicated, may hold values from -0.25 to 0.25
- w_out_dec: bfloat16 [512, 512], replicated, may hold values from -0.25 to 0.25
- grid_cot: bfloat16 [131072, 512], P(('band', 'mesh')), may hold values from -6 to 6
- enc_send: int32 [128, 3, 3, 128], P(('band', 'mesh')), may hold values from 0 to 1023
- enc_slot: int32 [8192, 32], P(('band', 'mesh')), may hold values from 0 to 1151, as said below
- enc_count: int32 [8192], P(('band', 'mesh')), may hold values from 1 to 32
- dec_send: int32 [128, 3, 3, 128], P(('band', 'mesh')), may hold values from 0 to 63
- dec_slot: int32 [131072, 3], P(('band', 'mesh')), may hold values from 0 to 1151, as said below
- dec_count: int32 [131072], P(('band', 'mesh')), may hold values from 1 to 3
Outputs:
- grid_grad: float32 [131072, 512], P(('band', 'mesh'))
- mesh_grad: float32 [8192, 512], P(('band', 'mesh'))
- grad_src_enc: float32 [512, 512], replicated
- grad_dst_enc: float32 [512, 512], replicated
- grad_out_enc: float32 [512, 512], replicated
- grad_src_dec: float32 [512, 512], replicated
- grad_dst_dec: float32 [512, 512], replicated
- grad_out_dec: float32 [512, 512], replicated
The draws below stay inside these ranges and needn't reach their ends.
Inputs may be any that keep to these rules, and one draw needn't show every extreme that they name: enc_send[p, a, e, c] is a row among device p's 1024 grid nodes; rows may repeat. `enc_slot`: a receive row s = (a * 3 + e) * 128 + c of the mesh node's device whose sender's band b + a - 1 exists (0 to 16 - 1). dec_send[p, a, e, c] is a row among device p's 64 mesh nodes; rows may repeat. `dec_slot`: a receive row s = (a * 3 + e) * 128 + c of the grid node's device whose sender's band b + a - 1 exists (0 to 16 - 1).
All inputs are finite; a program needn't handle non-finite values.
Results may differ from the reference program's by a relative error of at most 0.02.
Values may be sent and summed in bfloat16 or wider, within the bound.
No kernel may reach another device: no remote copies, remote signals or barrier semaphores. Data moves between devices by JAX's collectives and lax.ppermute only.
A program may use at most 128 MiB of HBM per device.

```python
import jax
import jax.numpy as jnp
from jax import lax

D = 512
GD = 1024
MD = 64
KE = 32
KD = 3
CAPE = 128
CAPD = 128
RECV_E = 1152
RECV_D = 1152
G = 131072
M = 8192
N_BAND = 16
N_MESH = 8
DEVICES = 128


def neighbour_slots(key, rows_dev, places, capacity):
    total = DEVICES * rows_dev
    key_lat, key_lon, key_place = jax.random.split(key, 3)
    band_of = jnp.arange(total, dtype=jnp.int32) // rows_dev // N_MESH
    lowest = (band_of == 0).astype(jnp.int32)
    highest = (band_of == N_BAND - 1).astype(jnp.int32)
    allowed = jnp.maximum(3 - lowest - highest, 1)
    lat = lowest[:, None] + jax.random.randint(key_lat, (total, places), 0, 6) % allowed[:, None]
    lon = jax.random.randint(key_lon, (total, places), 0, 3)
    place = jax.random.randint(key_place, (total, places), 0, capacity)
    return ((lat * 3 + lon) * capacity + place).astype(jnp.int32)


def draw_enc_slot(key, part):
    key = jax.random.fold_in(key, 11)
    return neighbour_slots(key, MD, KE, CAPE)


def draw_dec_slot(key, part):
    key = jax.random.fold_in(key, 12)
    return neighbour_slots(key, GD, KD, CAPD)


def plant(values, stream_key, low, high):
    longest = values.shape.index(max(values.shape))
    spots = []
    for shift in (0, 1):
        where = [jax.random.randint(jax.random.fold_in(stream_key, axis), (), 0, length) for axis, length in enumerate(values.shape)]
        where[longest] = (where[longest] + shift) % values.shape[longest]
        spots.append(tuple(where))
    return values.at[spots[0]].set(low).at[spots[1]].set(high)


def block_levels(stream_key, shape, pieces, low, largest):
    factor_of = 1.0
    for axis_at, parts in pieces:
        heights = jax.random.uniform(jax.random.fold_in(jax.random.fold_in(stream_key, 6), axis_at), (parts,), jnp.float32, low / len(pieces), largest / len(pieces))
        factor_of = factor_of * jnp.repeat(jnp.exp(heights), shape[axis_at] // parts).reshape((-1,) + (1,) * (len(shape) - 1 - axis_at))
    return factor_of


def centred(key, extent, scale, most, cuts=(), kind=jnp.bfloat16):
    values = jax.random.normal(key, extent, jnp.float32) * scale
    if len(cuts) > 0:
        values = block_levels(key, extent, cuts, -0.22, 0.18) * values
    return jnp.clip(values, min=-most, max=most).astype(kind)


def setup_inputs(seed: int = 0) -> dict:
    arg_keys = jax.random.split(jax.random.key(seed), 16)
    grid_latent = centred(arg_keys[0], (G, D), 1.0, 6.0, ((0, 128),))
    mesh_latent = centred(arg_keys[1], (M, D), 1.0, 6.0, ((0, 128),))
    w_src_enc = centred(arg_keys[2], (D, D), D ** -0.5, 0.25)
    w_dst_enc = centred(arg_keys[3], (D, D), D ** -0.5, 0.25)
    w_out_enc = centred(arg_keys[4], (D, D), D ** -0.5, 0.25)
    w_src_dec = centred(arg_keys[5], (D, D), D ** -0.5, 0.25)
    w_dst_dec = centred(arg_keys[6], (D, D), D ** -0.5, 0.25)
    w_out_dec = centred(arg_keys[7], (D, D), D ** -0.5, 0.25)
    grid_cot = centred(arg_keys[8], (G, D), 1.0, 6.0, ((0, 128),))
    enc_send = plant(jax.random.randint(arg_keys[9], (DEVICES, 3, 3, CAPE), 0, GD), jax.random.fold_in(arg_keys[9], 1), 0, GD - 1).astype(jnp.int32)
    enc_slot = draw_enc_slot(jax.random.fold_in(arg_keys[15], 71), 0)
    enc_count = plant(jax.random.randint(arg_keys[11], (M,), 1, KE + 1), jax.random.fold_in(arg_keys[11], 1), 1, KE).astype(jnp.int32)
    dec_send = plant(jax.random.randint(arg_keys[12], (DEVICES, 3, 3, CAPD), 0, MD), jax.random.fold_in(arg_keys[12], 1), 0, MD - 1).astype(jnp.int32)
    dec_slot = draw_dec_slot(jax.random.fold_in(arg_keys[15], 71), 0)
    dec_count = plant(jax.random.randint(arg_keys[14], (G,), 1, KD + 1), jax.random.fold_in(arg_keys[14], 1), 1, KD).astype(jnp.int32)
    return dict(grid_latent=grid_latent, mesh_latent=mesh_latent, w_src_enc=w_src_enc, w_dst_enc=w_dst_enc, w_out_enc=w_out_enc, w_src_dec=w_src_dec, w_dst_dec=w_dst_dec, w_out_dec=w_out_dec, grid_cot=grid_cot, enc_send=enc_send, enc_slot=enc_slot, enc_count=enc_count, dec_send=dec_send, dec_slot=dec_slot, dec_count=dec_count)


def silu_slope(values):
    squashed = jax.nn.sigmoid(values)
    return squashed * (1.0 + values * (1.0 - squashed))


def slot_table(send_rows, owner_rows):
    device_count = send_rows.shape[0]
    devices = jnp.arange(device_count, dtype=jnp.int32)
    band_of = devices // N_MESH
    lon_of = devices % N_MESH
    offsets = jnp.arange(3, dtype=jnp.int32) - 1
    peer_band = jnp.clip(band_of[:, None] + offsets[None, :], 0, N_BAND - 1)
    peer_lon = (lon_of[:, None] + offsets[None, :]) % N_MESH
    peers = (peer_band[:, :, None] * N_MESH + peer_lon[:, None, :]).astype(jnp.int32)
    flipped = send_rows[:, ::-1, ::-1, :]
    lat_pick = jnp.arange(3, dtype=jnp.int32)[None, :, None]
    lon_pick = jnp.arange(3, dtype=jnp.int32)[None, None, :]
    rows = flipped[peers, lat_pick, lon_pick]
    table = peers[:, :, :, None] * owner_rows + rows
    return table.reshape(device_count, -1).astype(jnp.int32)


def edge_weight(counts, fanout):
    places = jnp.arange(fanout, dtype=jnp.int32)[None, :]
    live = (places < counts[:, None]).astype(jnp.float32)
    return live / counts[:, None].astype(jnp.float32)


def forward_side(received, latent, slots, counts, w_source, w_target):
    source_proj = jnp.dot(received, w_source, preferred_element_type=jnp.float32)
    target_proj = jnp.dot(latent, w_target, preferred_element_type=jnp.float32)
    before = source_proj[slots] + target_proj[:, None, :]
    weights = edge_weight(counts, slots.shape[1])
    mean_msg = jnp.sum(jax.nn.silu(before) * weights[:, :, None], axis=1).astype(jnp.bfloat16)
    return before, weights, mean_msg


def backward_side(received, latent, slots, before, weights, upstream, w_source, w_target, slot_count):
    width = before.shape[2]
    d_before = (upstream[:, None, :] * weights[:, :, None] * silu_slope(before)).astype(jnp.bfloat16)
    target_sum = jnp.sum(d_before.astype(jnp.float32), axis=1).astype(jnp.bfloat16)
    target_grad = jnp.dot(latent.T, target_sum, preferred_element_type=jnp.float32)
    direct = jnp.dot(target_sum, w_target.T, preferred_element_type=jnp.float32)
    slot_sum = jax.ops.segment_sum(d_before.reshape(-1, width).astype(jnp.float32), slots.reshape(-1), num_segments=slot_count).astype(jnp.bfloat16)
    source_grad = jnp.dot(received.T, slot_sum, preferred_element_type=jnp.float32)
    sent_back = jnp.dot(slot_sum, w_source.T, preferred_element_type=jnp.float32).astype(jnp.bfloat16)
    return target_grad, direct, source_grad, sent_back


def reference(grid_latent, mesh_latent, w_src_enc, w_dst_enc, w_out_enc, w_src_dec, w_dst_dec, w_out_dec, grid_cot, enc_send, enc_slot, enc_count, dec_send, dec_slot, dec_count):
    width = grid_latent.shape[1]
    enc_table = slot_table(enc_send, GD)
    dec_table = slot_table(dec_send, MD)
    mesh_blocks = mesh_latent.reshape(DEVICES, MD, width)
    grid_blocks = grid_latent.reshape(DEVICES, GD, width)
    cot_blocks = grid_cot.reshape(DEVICES, GD, width)
    enc_slots = enc_slot.reshape(DEVICES, MD, KE)
    enc_counts = enc_count.reshape(DEVICES, MD)
    dec_slots = dec_slot.reshape(DEVICES, GD, KD)
    dec_counts = dec_count.reshape(DEVICES, GD)

    def encode(table, slots, counts, latent):
        received = grid_latent[table]
        before, weights, mean_msg = forward_side(received, latent, slots, counts, w_src_enc, w_dst_enc)
        return received, before, weights, mean_msg

    def new_mesh(operands):
        table, slots, counts, latent = operands
        mean_msg = encode(table, slots, counts, latent)[3]
        return (latent.astype(jnp.float32) + jnp.dot(mean_msg, w_out_enc, preferred_element_type=jnp.float32)).astype(jnp.bfloat16)

    mesh_new = lax.map(new_mesh, (enc_table, enc_slots, enc_counts, mesh_blocks)).reshape(DEVICES * MD, width)
    zero_square = jnp.zeros((width, width), jnp.float32)

    def decode_step(carry, operands):
        mesh_dnew, source_acc, target_acc, output_acc = carry
        table, slots, counts, latent, cotangent = operands
        received = mesh_new[table]
        before, weights, mean_msg = forward_side(received, latent, slots, counts, w_src_dec, w_dst_dec)
        upstream = jnp.dot(cotangent, w_out_dec.T, preferred_element_type=jnp.float32)
        output_acc = output_acc + jnp.dot(mean_msg.T, cotangent, preferred_element_type=jnp.float32)
        target_grad, direct, source_grad, sent_back = backward_side(received, latent, slots, before, weights, upstream, w_src_dec, w_dst_dec, RECV_D)
        mesh_dnew = mesh_dnew.at[table].add(sent_back.astype(jnp.float32))
        return (mesh_dnew, source_acc + source_grad, target_acc + target_grad, output_acc), cotangent.astype(jnp.float32) + direct

    start_dec = (jnp.zeros((DEVICES * MD, width), jnp.float32), zero_square, zero_square, zero_square)
    (mesh_dnew, grad_src_dec, grad_dst_dec, grad_out_dec), grid_part = lax.scan(decode_step, start_dec, (dec_table, dec_slots, dec_counts, grid_blocks, cot_blocks))
    dnew_blocks = mesh_dnew.reshape(DEVICES, MD, width)

    def encode_step(carry, operands):
        grid_acc, source_acc, target_acc, output_acc = carry
        table, slots, counts, latent, dnew = operands
        received, before, weights, mean_msg = encode(table, slots, counts, latent)
        dnew_round = dnew.astype(jnp.bfloat16)
        upstream = jnp.dot(dnew_round, w_out_enc.T, preferred_element_type=jnp.float32)
        output_acc = output_acc + jnp.dot(mean_msg.T, dnew_round, preferred_element_type=jnp.float32)
        target_grad, direct, source_grad, sent_back = backward_side(received, latent, slots, before, weights, upstream, w_src_enc, w_dst_enc, RECV_E)
        grid_acc = grid_acc.at[table].add(sent_back.astype(jnp.float32))
        return (grid_acc, source_acc + source_grad, target_acc + target_grad, output_acc), dnew + direct

    start_enc = (jnp.zeros((DEVICES * GD, width), jnp.float32), zero_square, zero_square, zero_square)
    (grid_acc, grad_src_enc, grad_dst_enc, grad_out_enc), mesh_part = lax.scan(encode_step, start_enc, (enc_table, enc_slots, enc_counts, mesh_blocks, dnew_blocks))
    grid_grad = grid_part.reshape(DEVICES * GD, width) + grid_acc
    mesh_grad = mesh_part.reshape(DEVICES * MD, width)
    return (grid_grad, mesh_grad, grad_src_enc, grad_dst_enc, grad_out_enc, grad_src_dec, grad_dst_dec, grad_out_dec)
```

```python
import functools

import jax
import jax.numpy as jnp
from jax import lax
from jax.experimental import pallas as pl
from jax.experimental.pallas import tpu as pltpu
from jax.sharding import PartitionSpec as P

D = 512
GD = 1024
MD = 64
KE = 32
KD = 3
CAP = 128
ROWS = CAP + 16
NEAR = 640
NB = 16
NM = 8
AXES = ("band", "mesh")
BF = jnp.bfloat16
F32 = jnp.float32
MIB = 1 << 20

NN = (((1,), (0,)), ((), ()))
NT = (((1,), (1,)), ((), ()))
TN = (((0,), (0,)), ((), ()))


def mm(a, b, dims=NN):
    return lax.dot_general(a, b, dims, preferred_element_type=F32)


def iota(shape, dim):
    return lax.broadcasted_iota(jnp.int32, shape, dim)


def one_hot(index, shape, dim):
    return jnp.where(iota(shape, dim) == index, 1.0, 0.0).astype(BF)


def call(body, outs, name, flops, scratch=(), vmem=28, smem_first=False, n_in=0):
    specs = None
    if smem_first:
        specs = [pl.BlockSpec(memory_space=pltpu.SMEM)] + [pl.BlockSpec(memory_space=pltpu.VMEM)] * (n_in - 1)
    kwargs = {} if specs is None else dict(in_specs=specs)
    return pl.pallas_call(
        body,
        out_shape=[jax.ShapeDtypeStruct(s, t) for s, t in outs],
        scratch_shapes=list(scratch),
        name=name,
        cost_estimate=pl.CostEstimate(flops=flops, bytes_accessed=4 * MIB, transcendentals=0),
        compiler_params=pltpu.CompilerParams(vmem_limit_bytes=vmem * MIB),
        **kwargs,
    )


def pick_rows(send_ref, table_ref, latent_ref, *outs):
    columns = send_ref[...].T
    table = table_ref[...].astype(F32)
    pad = jnp.zeros((16, D - CAP), BF)
    for e in range(3):
        hot = jnp.concatenate(
            [one_hot(columns[:, 3 * a + e : 3 * a + e + 1], (CAP, GD), 1) for a in range(3)], axis=0
        )
        rows = mm(hot, latent_ref[...]).astype(BF)
        for a in range(3):
            i = 3 * a + e
            outs[e][a, 0:CAP, :] = rows[a * CAP : (a + 1) * CAP]
            numbers = jnp.where(iota((16, CAP), 0) == 0, table[i : i + 1, :], 0.0).astype(BF)
            outs[e][a, CAP:ROWS, :] = jnp.concatenate([numbers, pad], axis=1)


def sigmoid(v):
    return 0.5 * jnp.tanh(0.5 * v) + 0.5


def enc_forward(up, down, left, right, own, slot, count, latent, w_src, w_dst, w_out,
                mean_out, slope_out, new_out, table_out, recv_out, proj):
    for e in range(3):
        recv_out[e * CAP : (e + 1) * CAP] = up[e, 0:CAP]
        recv_out[(6 + e) * CAP : (7 + e) * CAP] = down[e, 0:CAP]
        table_out[e : e + 1] = up[e, CAP:ROWS, 0:CAP].astype(F32)[0:1]
        table_out[6 + e : 7 + e] = down[e, CAP:ROWS, 0:CAP].astype(F32)[0:1]
        side = (left, own, right)[e]
        recv_out[(3 + e) * CAP : (4 + e) * CAP] = side[1, 0:CAP]
        table_out[3 + e : 4 + e] = side[1, CAP:ROWS, 0:CAP].astype(F32)[0:1]
    table_out[9:16] = jnp.zeros((7, CAP), F32)
    for a in range(3):
        part = slice(a * 384, (a + 1) * 384)
        proj[part] = mm(recv_out[part], w_src[...]).astype(BF)
    columns = slot[...].T
    counts = jnp.broadcast_to(count[...], (8, MD)).T[:, 0:1]
    inverse = 1.0 / counts.astype(F32)
    target = mm(latent[...], w_dst[...])
    total = jnp.zeros((MD, D), F32)
    for c in range(4):
        hot = jnp.concatenate(
            [one_hot(columns[:, k : k + 1], (MD, 9 * CAP), 1) for k in range(8 * c, 8 * c + 8)], axis=0
        )
        values = mm(hot, proj[...])
        for j in range(8):
            k = 8 * c + j
            pre = values[j * MD : (j + 1) * MD] + target
            weight = jnp.where(k < counts, inverse, 0.0)
            sig = sigmoid(pre)
            act = pre * sig
            total = total + act * weight
            slope_out[k] = ((sig + act * (1.0 - sig)) * weight).astype(BF)
    mean = total.astype(BF)
    mean_out[...] = mean
    new_out[...] = (latent[...].astype(F32) + mm(mean, w_out[...])).astype(BF)


def merge_index(table, slot, count, out):
    numbers = table[...].astype(BF)
    for k in range(KD):
        s = slot[k : k + 1, :]
        high, low = s >> 7, s & 127
        found = mm(numbers, one_hot(low, (CAP, GD), 0))
        value = jnp.sum(jnp.where(iota((16, GD), 0) == high, found, 0.0), axis=0, keepdims=True)
        out[k : k + 1, :] = high * MD + value.astype(jnp.int32)
    out[3:4, :] = count[...]
    out[4:8, :] = jnp.zeros((4, GD), jnp.int32)


def decoder(up, own, down, index, grid, cot, w_src, w_dst, w_out,
            mean_out, dst_out, slots_out, back0, back1, back2, proj, acc):
    proj[0:192] = mm(up[...], w_src[...]).astype(BF)
    proj[192:384] = mm(own[...], w_src[...]).astype(BF)
    proj[384:576] = mm(down[...], w_src[...]).astype(BF)
    proj[576:NEAR] = jnp.zeros((NEAR - 576, D), BF)
    step = 256
    for g in range(0, GD, step):
        rows = index[:, g : g + step]
        columns = rows.T
        counts = columns[:, 3:4]
        inverse = 1.0 / counts.astype(F32)
        target = mm(grid[g : g + step], w_dst[...])
        upstream = mm(cot[g : g + step], w_out[...], NT)
        total = jnp.zeros((step, D), F32)
        received = jnp.zeros((step, D), F32)
        parts = []
        hot = jnp.concatenate([one_hot(columns[:, k : k + 1], (step, NEAR), 1) for k in range(KD)], axis=0)
        values = mm(hot, proj[...])
        for k in range(KD):
            pre = values[k * step : (k + 1) * step] + target
            weight = jnp.where(k < counts, inverse, 0.0)
            sig = sigmoid(pre)
            act = pre * sig
            total = total + act * weight
            change = (upstream * weight * (sig + act * (1.0 - sig))).astype(BF)
            received = received + change.astype(F32)
            parts.append(change)
        mean_out[g : g + step] = total.astype(BF)
        dst_out[g : g + step] = received.astype(BF)
        hot = jnp.concatenate([one_hot(rows[k : k + 1], (9 * MD, step), 0) for k in range(KD)], axis=1)
        added = mm(hot, jnp.concatenate(parts, axis=0))
        if g == 0:
            acc[...] = added
        else:
            acc[...] += added
    slots = acc[...].astype(BF)
    slots_out[...] = slots
    back = mm(slots, w_src[...], NT).astype(BF)
    for a in range(3):
        for e, ref in enumerate((back0, back1, back2)):
            ref[a] = back[(3 * a + e) * MD : (3 * a + e + 1) * MD]


def owner_chunk(place, half, one, two):
    core = place[0] ^ half
    x, y = place[1], place[2]
    first = jnp.where(core == 0, y, x)
    second = jnp.where(core == 0, x, y)
    number = core * 16 + ((first + one) & 3) * 4 + ((second + two) & 3)
    return pl.multiple_of(number * 16, 16)


def pack(place, grads, keep, send):
    for half, ref in enumerate((keep, send)):
        for one in range(4):
            for two in range(4):
                at = owner_chunk(place, half, one, two)
                for m in range(3):
                    ref[one, two, m] = grads[m, pl.ds(at, 16), :].astype(BF)


def dec_grads(place, up, own, down, slots, grid, dst, mean, cot, w_dst, keep, send, part_out, grads):
    grads[0] = (
        mm(up[...], slots[0:192], TN) + mm(own[...], slots[192:384], TN) + mm(down[...], slots[384:576], TN)
    )
    grads[1] = mm(grid[...], dst[...], TN)
    grads[2] = mm(mean[...], cot[...], TN)
    pack(place, grads, keep, send)
    for g in range(0, GD, 256):
        part_out[g : g + 256] = cot[g : g + 256].astype(F32) + mm(dst[g : g + 256], w_dst[...], NT)


def enc_backward(up, own, down, slope, row, w_src, w_dst, w_out,
                 grad_out, dround_out, dst_out, slots_out, back0, back1, back2, change):
    total = up[...].astype(F32) + own[...].astype(F32) + down[...].astype(F32)
    rounded = total.astype(BF)
    dround_out[...] = rounded
    upstream = mm(rounded, w_out[...], NT)
    received = jnp.zeros((MD, D), F32)
    for k in range(KE):
        value = (upstream * slope[k].astype(F32)).astype(BF)
        change[k * MD : (k + 1) * MD] = value
        received = received + value.astype(F32)
    dst = received.astype(BF)
    dst_out[...] = dst
    for e, ref in enumerate((back0, back1, back2)):
        hot = jnp.concatenate(
            [one_hot(row[...] - (3 * a + e) * CAP, (CAP, KE * MD), 0) for a in range(3)], axis=0
        )
        slots = mm(hot, change[...]).astype(BF)
        back = mm(slots, w_src[...], NT).astype(BF)
        for a in range(3):
            i = 3 * a + e
            slots_out[i * CAP : (i + 1) * CAP] = slots[a * CAP : (a + 1) * CAP]
            ref[a] = back[a * CAP : (a + 1) * CAP]
    grad_out[...] = total + mm(dst, w_dst[...], NT)


def enc_grads(place, recv, slots, latent, dst, mean, dround, keep, send, grads):
    grads[0] = mm(recv[...], slots[...], TN)
    grads[1] = mm(latent[...], dst[...], TN)
    grads[2] = mm(mean[...], dround[...], TN)
    pack(place, grads, keep, send)


def put_rows(send, up, left, own, right, down, part, out):
    for g in range(0, GD, 256):
        hot = jnp.concatenate(
            [one_hot(send[i : i + 1, :] - g, (256, CAP), 0) for i in range(9)], axis=1
        )
        rows = [up[e] for e in range(3)] + [left[1], own[1], right[1]] + [down[e] for e in range(3)]
        out[g : g + 256] = part[g : g + 256] + mm(hot, jnp.concatenate(rows, axis=0))


def unpack(place, mine, other, *outs):
    for half, ref in enumerate((mine, other)):
        for one in range(4):
            for two in range(4):
                at = owner_chunk(place, half, -one, -two)
                for m in range(3):
                    outs[m][pl.ds(at, 16), :] = ref[one, two, m].astype(F32)


def mesh_shift(x, by):
    return lax.ppermute(x, "mesh", [(i, (i + by) % NM) for i in range(NM)])


def band_shift(x, by):
    return lax.ppermute(x, "band", [(i, i + by) for i in range(NB) if 0 <= i + by < NB])


def device(x, y, z, core):
    return (x * 4 + z) * NM + y * 2 + core


def torus_shift(x, stage, by):
    pairs = []
    for i in range(NB * NM):
        b, j = divmod(i, NM)
        at = [b // 4, j // 2, b % 4]
        core = j % 2
        axis = {1: 1 - core, 2: core, 3: 2}[stage]
        to = list(at)
        to[axis] = (to[axis] + by) % 4
        pairs.append((i, device(*to, core)))
    return lax.ppermute(x, AXES, pairs)


def core_swap(x):
    pairs = [(i, i ^ 1) for i in range(NB * NM)]
    return lax.ppermute(x, AXES, pairs)


def add(*values):
    total = values[0].astype(F32)
    for v in values[1:]:
        total = total + v.astype(F32)
    return total.astype(BF)


def all_sum(keep, send):
    got = core_swap(send)
    s = [add(keep[d], got[d]) for d in range(4)]
    got = [torus_shift(s[d], 1, d) for d in (1, 2, 3)]
    s = [add(s[0][d], *(g[d] for g in got)) for d in range(4)]
    got = [torus_shift(s[d], 2, d) for d in (1, 2, 3)]
    v = add(s[0], *got)
    one, two, three = (torus_shift(v, 3, d) for d in (1, 2, 3))
    v = ((v.astype(F32) + two.astype(F32)) + (one.astype(F32) + three.astype(F32))).astype(BF)
    v = jnp.stack([v] + [torus_shift(v, 2, d) for d in (1, 2, 3)])
    v = jnp.stack([v] + [torus_shift(v, 1, d) for d in (1, 2, 3)])
    return v, core_swap(v)


def exchange(x0, x1, x2):
    left = mesh_shift(x2, 1)
    right = mesh_shift(x0, -1)
    up = band_shift(jnp.stack([left[2], x1[2], right[2]]), 1)
    down = band_shift(jnp.stack([left[0], x1[0], right[0]]), -1)
    return up, left, right, down


def body(grid_latent, mesh_latent, w_src_enc, w_dst_enc, w_out_enc, w_src_dec, w_dst_dec, w_out_dec, grid_cot,
         enc_send, enc_slot, enc_count, dec_send, dec_slot, dec_count):
    b, j = lax.axis_index("band"), lax.axis_index("mesh")
    place = jnp.stack([j % 2, b // 4, j // 2, b % 4]).astype(jnp.int32)
    send_index = jnp.pad(enc_send.reshape(9, CAP), ((0, 7), (0, 0)))
    send_table = jnp.pad(dec_send.reshape(9, CAP), ((0, 7), (0, 0)))
    slot_rows = enc_slot.T
    slot_line = slot_rows.reshape(1, KE * MD)

    block = ((3, ROWS, D), BF)
    x0, x1, x2 = call(pick_rows, [block] * 3, "pick_rows", 1300000000)(send_index, send_table, grid_latent)
    up, left, right, down = exchange(x0, x1, x2)
    mean_enc, slope, mesh_new, table, recv = call(
        enc_forward,
        [((MD, D), BF), ((KE, MD, D), BF), ((MD, D), BF), ((16, CAP), F32), ((9 * CAP, D), BF)],
        "enc_forward", 3400000000, scratch=[pltpu.VMEM((9 * CAP, D), BF)],
    )(up, down, left, right, x1, slot_rows, enc_count.reshape(1, MD), mesh_latent, w_src_enc, w_dst_enc, w_out_enc)

    up = band_shift(mesh_new, 1)
    down = band_shift(mesh_new, -1)
    (index,) = call(merge_index, [((8, GD), jnp.int32)], "merge_index", 100000000)(
        table, dec_slot.T, dec_count.reshape(1, GD)
    )
    mine = jnp.stack([up, mesh_new, down])
    left = mesh_shift(mine, 1)
    right = mesh_shift(mine, -1)
    near = [jnp.concatenate([left[a], mine[a], right[a]], axis=0) for a in range(3)]

    rows = ((GD, D), BF)
    mean_dec, dst_dec, slots_dec, b0, b1, b2 = call(
        decoder,
        [rows, rows, ((9 * MD, D), BF)] + [((3, MD, D), BF)] * 3,
        "decoder", 5500000000,
        scratch=[pltpu.VMEM((NEAR, D), BF), pltpu.VMEM((9 * MD, D), F32)],
    )(*near, index, grid_latent, grid_cot, w_src_dec, w_dst_dec, w_out_dec)

    left = mesh_shift(b2, 1)
    right = mesh_shift(b0, -1)
    sums = [left[a].astype(F32) + b1[a].astype(F32) + right[a].astype(F32) for a in range(3)]
    up = band_shift(sums[2].astype(BF), 1)
    down = band_shift(sums[0].astype(BF), -1)

    half = ((4, 4, 3, 16, D), BF)
    keep, send, grid_part = call(
        dec_grads, [half, half, ((GD, D), F32)], "dec_grads", 2300000000,
        scratch=[pltpu.VMEM((3, D, D), F32)], smem_first=True, n_in=10,
    )(place, *near, slots_dec, grid_latent, dst_dec, mean_dec, grid_cot, w_dst_dec)

    mesh_grad, dround, dst_enc, slots_enc, x0, x1, x2 = call(
        enc_backward,
        [((MD, D), F32), ((MD, D), BF), ((MD, D), BF), ((9 * CAP, D), BF)] + [((3, CAP, D), BF)] * 3,
        "enc_backward", 3200000000, scratch=[pltpu.VMEM((KE * MD, D), BF)],
    )(up, sums[1], down, slope, slot_line, w_src_enc, w_dst_enc, w_out_enc)
    keep_enc, send_enc = call(
        enc_grads, [half, half], "enc_grads", 700000000, scratch=[pltpu.VMEM((3, D, D), F32)],
        smem_first=True, n_in=7,
    )(place, recv, slots_enc, mesh_latent, dst_enc, mean_enc, dround)

    up, left, right, down = exchange(x0, x1, x2)
    (grid_grad,) = call(put_rows, [((GD, D), F32)], "put_rows", 1300000000)(
        send_index, up, left, x1, right, down, grid_part
    )
    square = ((D, D), F32)
    spread = functools.partial(call, unpack, [square] * 3, smem_first=True, n_in=3)
    dec = spread("unpack_dec", 1000000)(place, *all_sum(keep, send))
    enc = spread("unpack_enc", 1000000)(place, *all_sum(keep_enc, send_enc))
    return (grid_grad, mesh_grad, *enc, *dec)


def solution(mesh):
    rows = P(AXES, None)
    whole = P()
    return jax.shard_map(
        body,
        mesh=mesh,
        in_specs=(rows, rows) + (whole,) * 6 + (rows, P(AXES, None, None, None), rows, P(AXES),
                                               P(AXES, None, None, None), rows, P(AXES)),
        out_specs=(rows, rows) + (whole,) * 6,
        check_vma=False,
    )
```

```python
import functools

import jax
import jax.numpy as jnp
from jax import lax
from jax.experimental import pallas as pl
from jax.experimental.pallas import tpu as pltpu
from jax.sharding import PartitionSpec as P

D = 512
GD = 1024
MD = 64
KE = 32
KD = 3
CAP = 128
ROWS = CAP + 16
NEAR = 640
NB = 16
NM = 8
AXES = ("band", "mesh")
BF = jnp.bfloat16
F32 = jnp.float32
MIB = 1 << 20

NN = (((1,), (0,)), ((), ()))
NT = (((1,), (1,)), ((), ()))
TN = (((0,), (0,)), ((), ()))


def mm(a, b, dims=NN):
    return lax.dot_general(a, b, dims, preferred_element_type=F32)


def iota(shape, dim):
    return lax.broadcasted_iota(jnp.int32, shape, dim)


def one_hot(index, shape, dim):
    return jnp.where(iota(shape, dim) == index, 1.0, 0.0).astype(BF)


def place():
    b, j = lax.axis_index("band"), lax.axis_index("mesh")
    return j & 1, b >> 2, j >> 1, b & 1


def own_number(block):
    core, _, _, odd = place()
    a = (block * 11) >> 5
    e = block - 3 * a
    return 3 * jnp.where(odd == 1, 2 - a, a) + jnp.where(core == 1, 2 - e, e)


def own_slot(slot):
    return (own_number(slot >> 7) << 7) | (slot & 127)


def call(body, outs, name, flops, scratch=(), vmem=28, in_place=False):
    kwargs = dict(out_specs=[pl.BlockSpec(memory_space=pl.ANY)] * len(outs)) if in_place else {}
    return pl.pallas_call(
        body,
        out_shape=[jax.ShapeDtypeStruct(s, t) for s, t in outs],
        scratch_shapes=list(scratch),
        name=name,
        cost_estimate=pl.CostEstimate(flops=flops, bytes_accessed=4 * MIB, transcendentals=0),
        compiler_params=pltpu.CompilerParams(vmem_limit_bytes=vmem * MIB),
        **kwargs,
    )


def pick_rows(send_ref, latent_ref, *outs):
    columns = send_ref[0:16].T
    table = send_ref[16:32].astype(F32)
    pad = jnp.zeros((16, D - CAP), BF)
    for e in range(3):
        hot = jnp.concatenate(
            [one_hot(columns[:, 3 * a + e : 3 * a + e + 1], (CAP, GD), 1) for a in range(3)], axis=0
        )
        rows = mm(hot, latent_ref[...]).astype(BF)
        for a in range(3):
            i = 3 * a + e
            outs[e][a, 0:CAP, :] = rows[a * CAP : (a + 1) * CAP]
            numbers = jnp.where(iota((16, CAP), 0) == 0, table[i : i + 1, :], 0.0).astype(BF)
            outs[e][a, CAP:ROWS, :] = jnp.concatenate([numbers, pad], axis=1)


def sigmoid(v):
    return 0.5 * jnp.tanh(0.5 * v) + 0.5


def enc_forward(up, down, left, right, own, slot, count, latent, w_src, w_dst, w_out,
                mean_out, slope_out, new_out, table_out, recv_out, proj):
    for e in range(3):
        recv_out[e * CAP : (e + 1) * CAP] = up[e, 0:CAP]
        recv_out[(6 + e) * CAP : (7 + e) * CAP] = down[e, 0:CAP]
        table_out[e : e + 1] = up[e, CAP:ROWS, 0:CAP].astype(F32)[0:1]
        table_out[6 + e : 7 + e] = down[e, CAP:ROWS, 0:CAP].astype(F32)[0:1]
        side = (left, own, right)[e]
        recv_out[(3 + e) * CAP : (4 + e) * CAP] = side[1, 0:CAP]
        table_out[3 + e : 4 + e] = side[1, CAP:ROWS, 0:CAP].astype(F32)[0:1]
    table_out[9:16] = jnp.zeros((7, CAP), F32)
    for a in range(3):
        part = slice(a * 384, (a + 1) * 384)
        proj[part] = mm(recv_out[part], w_src[...]).astype(BF)
    columns = own_slot(slot[...]).T
    counts = jnp.broadcast_to(count[...], (8, MD)).T[:, 0:1]
    inverse = 1.0 / counts.astype(F32)
    target = mm(latent[...], w_dst[...])
    total = jnp.zeros((MD, D), F32)
    for c in range(4):
        hot = jnp.concatenate(
            [one_hot(columns[:, k : k + 1], (MD, 9 * CAP), 1) for k in range(8 * c, 8 * c + 8)], axis=0
        )
        values = mm(hot, proj[...])
        for j in range(8):
            k = 8 * c + j
            pre = values[j * MD : (j + 1) * MD] + target
            weight = jnp.where(k < counts, inverse, 0.0)
            sig = sigmoid(pre)
            act = pre * sig
            total = total + act * weight
            slope_out[k] = ((sig + act * (1.0 - sig)) * weight).astype(BF)
    mean = total.astype(BF)
    mean_out[...] = mean
    new_out[...] = (latent[...].astype(F32) + mm(mean, w_out[...])).astype(BF)


def merge_index(table, slot, count, enc_slot, out, line_out):
    own = own_slot(enc_slot[...])
    for k in range(0, KE, 2):
        line_out[:, k * MD : (k + 2) * MD] = jnp.concatenate([own[k : k + 1], own[k + 1 : k + 2]], axis=1)
    numbers = table[...].astype(BF)
    for k in range(KD):
        s = slot[k : k + 1, :]
        high, low = own_number(s >> 7), s & 127
        found = mm(numbers, one_hot(low, (CAP, GD), 0))
        value = jnp.sum(jnp.where(iota((16, GD), 0) == high, found, 0.0), axis=0, keepdims=True)
        out[k : k + 1, :] = high * MD + value.astype(jnp.int32)
    out[3:4, :] = count[...]
    out[4:8, :] = jnp.zeros((4, GD), jnp.int32)


def decoder(up, own, down, index, grid, cot, w_src, w_dst, w_out,
            mean_out, dst_out, slots_out, back0, back1, back2, proj, acc):
    proj[0:192] = mm(up[...], w_src[...]).astype(BF)
    proj[192:384] = mm(own[...], w_src[...]).astype(BF)
    proj[384:576] = mm(down[...], w_src[...]).astype(BF)
    proj[576:NEAR] = jnp.zeros((NEAR - 576, D), BF)
    step = 256
    for g in range(0, GD, step):
        rows = index[:, g : g + step]
        columns = rows.T
        counts = columns[:, 3:4]
        inverse = 1.0 / counts.astype(F32)
        target = mm(grid[g : g + step], w_dst[...])
        upstream = mm(cot[g : g + step], w_out[...], NT)
        total = jnp.zeros((step, D), F32)
        received = jnp.zeros((step, D), F32)
        parts = []
        hot = jnp.concatenate([one_hot(columns[:, k : k + 1], (step, NEAR), 1) for k in range(KD)], axis=0)
        values = mm(hot, proj[...])
        for k in range(KD):
            pre = values[k * step : (k + 1) * step] + target
            weight = jnp.where(k < counts, inverse, 0.0)
            sig = sigmoid(pre)
            act = pre * sig
            total = total + act * weight
            change = (upstream * weight * (sig + act * (1.0 - sig))).astype(BF)
            received = received + change.astype(F32)
            parts.append(change)
        mean_out[g : g + step] = total.astype(BF)
        dst_out[g : g + step] = received.astype(BF)
        hot = jnp.concatenate([one_hot(rows[k : k + 1], (9 * MD, step), 0) for k in range(KD)], axis=1)
        added = mm(hot, jnp.concatenate(parts, axis=0))
        if g == 0:
            acc[...] = added
        else:
            acc[...] += added
    slots = acc[...].astype(BF)
    slots_out[...] = slots
    back = mm(slots, w_src[...], NT).astype(BF)
    for a in range(3):
        for e, ref in enumerate((back0, back1, back2)):
            ref[a] = back[(3 * a + e) * MD : (3 * a + e + 1) * MD]


def owner_chunk(half, one, two):
    core, x, y, _ = place()
    core = core ^ half
    first = jnp.where(core == 0, y, x)
    second = jnp.where(core == 0, x, y)
    number = core * 16 + ((first + one) & 3) * 4 + ((second + two) & 3)
    return pl.multiple_of(number * 16, 16)


def pack(grads, keep, send):
    for half, ref in enumerate((keep, send)):
        for one in range(4):
            for two in range(4):
                at = owner_chunk(half, one, two)
                for m in range(3):
                    ref[one, two, m] = grads[m, pl.ds(at, 16), :].astype(BF)


def dec_grads(up, own, down, slots, grid, dst, mean, cot, w_dst, keep, send, part_out, grads):
    grads[0] = (
        mm(up[...], slots[0:192], TN) + mm(own[...], slots[192:384], TN) + mm(down[...], slots[384:576], TN)
    )
    grads[1] = mm(grid[...], dst[...], TN)
    grads[2] = mm(mean[...], cot[...], TN)
    pack(grads, keep, send)
    for g in range(0, GD, 256):
        part_out[g : g + 256] = cot[g : g + 256].astype(F32) + mm(dst[g : g + 256], w_dst[...], NT)


def enc_backward(up, own, down, slope, row, w_src, w_dst, w_out,
                 grad_out, dround_out, dst_out, slots_out, back0, back1, back2, change):
    total = up[...].astype(F32) + own[...].astype(F32) + down[...].astype(F32)
    rounded = total.astype(BF)
    dround_out[...] = rounded
    upstream = mm(rounded, w_out[...], NT)
    received = jnp.zeros((MD, D), F32)
    for k in range(KE):
        value = (upstream * slope[k].astype(F32)).astype(BF)
        change[k * MD : (k + 1) * MD] = value
        received = received + value.astype(F32)
    dst = received.astype(BF)
    dst_out[...] = dst
    line = row[...]
    for e, ref in enumerate((back0, back1, back2)):
        hot = jnp.concatenate(
            [one_hot(line - (3 * a + e) * CAP, (CAP, KE * MD), 0) for a in range(3)], axis=0
        )
        slots = mm(hot, change[...]).astype(BF)
        back = mm(slots, w_src[...], NT).astype(BF)
        for a in range(3):
            i = 3 * a + e
            slots_out[i * CAP : (i + 1) * CAP] = slots[a * CAP : (a + 1) * CAP]
            ref[a] = back[a * CAP : (a + 1) * CAP]
    grad_out[...] = total + mm(dst, w_dst[...], NT)


def enc_grads(recv, slots, latent, dst, mean, dround, keep, send, grads):
    grads[0] = mm(recv[...], slots[...], TN)
    grads[1] = mm(latent[...], dst[...], TN)
    grads[2] = mm(mean[...], dround[...], TN)
    pack(grads, keep, send)


def put_rows(send, up, left, own, right, down, part, out):
    for g in range(0, GD, 256):
        hot = jnp.concatenate(
            [one_hot(send[i : i + 1, :] - g, (256, CAP), 0) for i in range(9)], axis=1
        )
        rows = [up[e] for e in range(3)] + [left[1], own[1], right[1]] + [down[e] for e in range(3)]
        out[g : g + 256] = part[g : g + 256] + mm(hot, jnp.concatenate(rows, axis=0))


def unpack(mine, other, *refs):
    outs, (whole, sems) = refs[:6], refs[6:]
    copies = [pltpu.make_async_copy(whole.at[m], outs[m], sems.at[m]) for m in range(6)]
    for m in range(6):
        for half, ref in enumerate((mine, other)):
            for one in range(4):
                for two in range(4):
                    whole[m, pl.ds(owner_chunk(half, -one, -two), 16), :] = ref[one, two, m].astype(F32)
        copies[m].start()
    for copy in copies:
        copy.wait()


def pairs(x, partner):
    return lax.ppermute(x, AXES, [(i, partner(i)) for i in range(NB * NM) if partner(i) is not None])


def other_core(x):
    return pairs(x, lambda i: i ^ 1)


def other_chip(x):
    return pairs(x, lambda i: i // NM * NM + (i % NM + (1 if i % 2 else -1)) % NM)


def near_band(x):
    return pairs(x, lambda i: i ^ NM)


def far_band(x):
    def partner(i):
        to = i + (NM if i // NM % 2 else -NM)
        return to if 0 <= to < NB * NM else None

    return pairs(x, partner)


def device(x, y, z, core):
    return (x * 4 + z) * NM + y * 2 + core


def torus_shift(x, stage, by):
    def partner(i):
        b, j = divmod(i, NM)
        at = [b // 4, j // 2, b % 4]
        axis = {1: 1 - j % 2, 2: j % 2, 3: 2}[stage]
        at[axis] = (at[axis] + by) % 4
        return device(*at, j % 2)

    return pairs(x, partner)


def add(*values):
    total = values[0].astype(F32)
    for v in values[1:]:
        total = total + v.astype(F32)
    return total.astype(BF)


def scatter_sum(*packed):
    got = [other_core(send) for _, send in packed]
    s = [jnp.concatenate([add(keep[d], g[d]) for (keep, _), g in zip(packed, got)], axis=1) for d in range(4)]
    got = [torus_shift(s[d], 1, d) for d in (1, 2, 3)]
    return [add(s[0][d], *(g[d] for g in got)) for d in range(4)]


def second_sum(s):
    got = [torus_shift(s[d], 2, d) for d in (1, 2, 3)]
    return add(s[0], *got)


def spread_sum(v):
    one, two, three = (torus_shift(v, 3, d) for d in (1, 2, 3))
    v = ((v.astype(F32) + two.astype(F32)) + (one.astype(F32) + three.astype(F32))).astype(BF)
    v = jnp.stack([v] + [torus_shift(v, 2, d) for d in (1, 2, 3)])
    v = jnp.stack([v] + [torus_shift(v, 1, d) for d in (1, 2, 3)])
    return v, other_core(v)


def first_exchange(x0, x1, x2):
    return other_chip(x0), x1, other_core(x2)


def second_exchange(left, own, right):
    up = far_band(jnp.stack([left[0], own[0], right[0]]))
    down = near_band(jnp.stack([left[2], own[2], right[2]]))
    return up, down


def body(grid_latent, mesh_latent, w_src_enc, w_dst_enc, w_out_enc, w_src_dec, w_dst_dec, w_out_dec, grid_cot,
         enc_send, enc_slot, enc_count, dec_send, dec_slot, dec_count):
    core, _, _, odd = place()
    sends = jnp.concatenate([enc_send, dec_send], axis=0)
    sends = jnp.where(odd == 1, sends[:, ::-1], sends)
    sends = jnp.where(core == 1, sends[:, :, ::-1], sends)
    sends = jnp.pad(sends.reshape(2, 9, CAP), ((0, 0), (0, 7), (0, 0))).reshape(32, CAP)
    slot_rows = enc_slot.T

    block = ((3, ROWS, D), BF)
    x0, x1, x2 = call(pick_rows, [block] * 3, "pick_rows", 1300000000)(sends, grid_latent)
    left, _, right = first_exchange(x0, x1, x2)
    up, down = second_exchange(left, x1, right)
    mean_enc, slope, mesh_new, table, recv = call(
        enc_forward,
        [((MD, D), BF), ((KE, MD, D), BF), ((MD, D), BF), ((16, CAP), F32), ((9 * CAP, D), BF)],
        "enc_forward", 3400000000, scratch=[pltpu.VMEM((9 * CAP, D), BF)],
    )(up, down, left, right, x1, slot_rows, enc_count.reshape(1, MD), mesh_latent, w_src_enc, w_dst_enc, w_out_enc)

    up = far_band(mesh_new)
    down = near_band(mesh_new)
    index, slot_line = call(
        merge_index, [((8, GD), jnp.int32), ((1, KE * MD), jnp.int32)], "merge_index", 100000000
    )(table, dec_slot.T, dec_count.reshape(1, GD), slot_rows)
    mine = jnp.stack([up, mesh_new, down])
    left = other_chip(mine)
    right = other_core(mine)
    near = [jnp.concatenate([left[a], mine[a], right[a]], axis=0) for a in range(3)]

    rows = ((GD, D), BF)
    mean_dec, dst_dec, slots_dec, b0, b1, b2 = call(
        decoder,
        [rows, rows, ((9 * MD, D), BF)] + [((3, MD, D), BF)] * 3,
        "decoder", 5500000000,
        scratch=[pltpu.VMEM((NEAR, D), BF), pltpu.VMEM((9 * MD, D), F32)],
    )(*near, index, grid_latent, grid_cot, w_src_dec, w_dst_dec, w_out_dec)

    left = other_chip(b0)
    right = other_core(b2)
    sums = [left[a].astype(F32) + b1[a].astype(F32) + right[a].astype(F32) for a in range(3)]
    up = far_band(sums[0].astype(BF))
    down = near_band(sums[2].astype(BF))

    half = ((4, 4, 3, 16, D), BF)
    *packed_dec, grid_part = call(
        dec_grads, [half, half, ((GD, D), F32)], "dec_grads", 2300000000, scratch=[pltpu.VMEM((3, D, D), F32)],
    )(*near, slots_dec, grid_latent, dst_dec, mean_dec, grid_cot, w_dst_dec)

    mesh_grad, dround, dst_enc, slots_enc, x0, x1, x2 = call(
        enc_backward,
        [((MD, D), F32), ((MD, D), BF), ((MD, D), BF), ((9 * CAP, D), BF)] + [((3, CAP, D), BF)] * 3,
        "enc_backward", 3200000000, scratch=[pltpu.VMEM((KE * MD, D), BF)],
    )(up, sums[1], down, slope, slot_line, w_src_enc, w_dst_enc, w_out_enc)
    packed_enc = call(
        enc_grads, [half, half], "enc_grads", 700000000, scratch=[pltpu.VMEM((3, D, D), F32)],
    )(recv, slots_enc, mesh_latent, dst_enc, mean_enc, dround)

    left, _, right = first_exchange(x0, x1, x2)
    part_sums = scatter_sum(packed_enc, packed_dec)
    part_sums, left, right = lax.optimization_barrier((part_sums, left, right))
    up, down = second_exchange(left, x1, right)
    part_sum = second_sum(part_sums)
    part_sum, up, down = lax.optimization_barrier((part_sum, up, down))
    (grid_grad,) = call(put_rows, [((GD, D), F32)], "put_rows", 1300000000)(
        sends, up, left, x1, right, down, grid_part
    )
    grads = call(
        unpack, [((D, D), F32)] * 6, "unpack", 1000000,
        scratch=[pltpu.VMEM((6, D, D), F32), pltpu.SemaphoreType.DMA((6,))], in_place=True,
    )(*spread_sum(part_sum))
    return (grid_grad, mesh_grad, *grads)


def solution(mesh):
    rows = P(AXES, None)
    whole = P()
    return jax.shard_map(
        body,
        mesh=mesh,
        in_specs=(rows, rows) + (whole,) * 6 + (rows, P(AXES, None, None, None), rows, P(AXES),
                                               P(AXES, None, None, None), rows, P(AXES)),
        out_specs=(rows, rows) + (whole,) * 6,
        check_vma=False,
    )
```

```python
import functools

import jax
import jax.numpy as jnp
from jax import lax
from jax.experimental import pallas as pl
from jax.experimental.pallas import tpu as pltpu
from jax.sharding import PartitionSpec as P

D = 512
GD = 1024
MD = 64
KE = 32
KD = 3
CAP = 128
ROWS = CAP + 16
NEAR = 640
STEP = 256
NB = 16
NM = 8
AXES = ("band", "mesh")
BF = jnp.bfloat16
F32 = jnp.float32
MIB = 1 << 20

NN = (((1,), (0,)), ((), ()))
NT = (((1,), (1,)), ((), ()))
TN = (((0,), (0,)), ((), ()))


def mm(a, b, dims=NN):
    return lax.dot_general(a, b, dims, preferred_element_type=F32)


def iota(shape, dim):
    return lax.broadcasted_iota(jnp.int32, shape, dim)


def one_hot(index, shape, dim):
    return jnp.where(iota(shape, dim) == index, 1.0, 0.0).astype(BF)


def place():
    b, j = lax.axis_index("band"), lax.axis_index("mesh")
    return j & 1, b >> 2, j >> 1, b & 3


def own_number(block):
    core, _, _, z = place()
    odd = z & 1
    a = (block * 11) >> 5
    e = block - 3 * a
    return 3 * jnp.where(odd == 1, 2 - a, a) + jnp.where(core == 1, 2 - e, e)


def own_slot(slot):
    return (own_number(slot >> 7) << 7) | (slot & 127)


def call(body, outs, name, flops, scratch=(), vmem=16, **kwargs):
    return pl.pallas_call(
        body,
        out_shape=[jax.ShapeDtypeStruct(s, t) for s, t in outs],
        scratch_shapes=list(scratch),
        name=name,
        cost_estimate=pl.CostEstimate(flops=flops, bytes_accessed=4 * MIB, transcendentals=0),
        compiler_params=pltpu.CompilerParams(vmem_limit_bytes=vmem * MIB),
        **kwargs,
    )


def pick_rows(send_ref, latent_ref, left, own0, own1, own2, right):
    columns = send_ref[0:16].T
    table = send_ref[16:32].astype(F32)
    pad = jnp.zeros((16, D - CAP), BF)
    for e in range(3):
        hot = jnp.concatenate(
            [one_hot(columns[:, 3 * a + e : 3 * a + e + 1], (CAP, GD), 1) for a in range(3)], axis=0
        )
        rows = mm(hot, latent_ref[...]).astype(BF)
        for a in range(3):
            i = 3 * a + e
            out = (left.at[a], (own0, own1, own2)[a], right.at[a])[e]
            out[0:CAP, :] = rows[a * CAP : (a + 1) * CAP]
            numbers = jnp.where(iota((16, CAP), 0) == 0, table[i : i + 1, :], 0.0).astype(BF)
            out[CAP:ROWS, :] = jnp.concatenate([numbers, pad], axis=1)


def sigmoid(v):
    return 0.5 * jnp.tanh(0.5 * v) + 0.5


def prepare(slot, grid, cot, w_dst, w_out, hot_out, back_out, target_out, up_out):
    own = own_slot(slot[...])
    columns = own.T
    for k in range(KE):
        hot_out[k * MD : (k + 1) * MD] = one_hot(columns[:, k : k + 1], (MD, 9 * CAP), 1)
    for k in range(0, KE, 2):
        line = jnp.concatenate([own[k : k + 1], own[k + 1 : k + 2]], axis=1)
        back_out[:, k * MD : (k + 2) * MD] = one_hot(line, (9 * CAP, 2 * MD), 0)
    for g in range(0, GD, 256):
        target_out[g : g + 256] = mm(grid[g : g + 256], w_dst[...])
        up_out[g : g + 256] = mm(cot[g : g + 256], w_out[...], NT)


def enc_forward(up, up2, down, down2, left, right, own, hot, count, latent, w_src, w_dst, w_out,
                mean_out, slope_out, new_out, table_out, recv_out, proj):
    blocks = (up2.at[0], up, up2.at[1], left.at[1], own, right.at[1], down2.at[0], down, down2.at[1])
    for i, block in enumerate(blocks):
        recv_out[i * CAP : (i + 1) * CAP] = block[0:CAP]
        table_out[i : i + 1] = block[CAP:ROWS, 0:CAP].astype(F32)[0:1]
    table_out[9:16] = jnp.zeros((7, CAP), F32)
    for a in range(3):
        part = slice(a * 384, (a + 1) * 384)
        proj[part] = mm(recv_out[part], w_src[...]).astype(BF)
    counts = jnp.broadcast_to(count[...], (8, MD)).T[:, 0:1]
    inverse = 1.0 / counts.astype(F32)
    target = mm(latent[...], w_dst[...])
    total = jnp.zeros((MD, D), F32)
    for c in range(4):
        values = mm(hot[c * 8 * MD : (c + 1) * 8 * MD], proj[...])
        for j in range(8):
            k = 8 * c + j
            pre = values[j * MD : (j + 1) * MD] + target
            weight = jnp.where(k < counts, inverse, 0.0)
            sig = sigmoid(pre)
            act = pre * sig
            total = total + act * weight
            slope_out[k] = ((sig + act * (1.0 - sig)) * weight).astype(BF)
    mean = total.astype(BF)
    mean_out[...] = mean
    new_out[...] = (latent[...].astype(F32) + mm(mean, w_out[...])).astype(BF)


def merge_index(table, slot, hot_out, back_out):
    numbers = table[...].astype(BF)
    for k in range(KD):
        s = slot[k : k + 1, :]
        high, low = own_number(s >> 7), s & 127
        found = mm(numbers, one_hot(low, (CAP, GD), 0))
        value = jnp.sum(jnp.where(iota((16, GD), 0) == high, found, 0.0), axis=0, keepdims=True)
        row = high * MD + value.astype(jnp.int32)
        column = jnp.broadcast_to(row, (8, GD)).T[:, 0:1]
        for c in range(4):
            part = slice(c * STEP, (c + 1) * STEP)
            hot_out[c, k * STEP : (k + 1) * STEP] = one_hot(column[part], (STEP, NEAR), 1)
            back_out[c, :, k * STEP : (k + 1) * STEP] = one_hot(row[:, part], (9 * MD, STEP), 0)


def decoder(up, own, down, hot, back_hot, count, target, upstream, w_src,
            mean_out, dst_out, slots_out, back0, back1, back2, proj, acc):
    proj[0:192] = mm(up[...], w_src[...]).astype(BF)
    proj[192:384] = mm(own[...], w_src[...]).astype(BF)
    proj[384:576] = mm(down[...], w_src[...]).astype(BF)
    proj[576:NEAR] = jnp.zeros((NEAR - 576, D), BF)
    for c in range(4):
        part = slice(c * STEP, (c + 1) * STEP)
        counts = jnp.broadcast_to(count[:, part], (8, STEP)).T[:, 0:1]
        inverse = 1.0 / counts.astype(F32)
        total = jnp.zeros((STEP, D), F32)
        received = jnp.zeros((STEP, D), F32)
        parts = []
        values = mm(hot[c], proj[...])
        for k in range(KD):
            pre = values[k * STEP : (k + 1) * STEP] + target[part]
            weight = jnp.where(k < counts, inverse, 0.0)
            sig = sigmoid(pre)
            act = pre * sig
            total = total + act * weight
            change = (upstream[part] * weight * (sig + act * (1.0 - sig))).astype(BF)
            received = received + change.astype(F32)
            parts.append(change)
        mean_out[part] = total.astype(BF)
        dst_out[part] = received.astype(BF)
        added = mm(back_hot[c], jnp.concatenate(parts, axis=0))
        if c == 0:
            acc[...] = added
        else:
            acc[...] += added
    slots = acc[...].astype(BF)
    slots_out[...] = slots
    back = mm(slots, w_src[...], NT).astype(BF)
    for a in range(3):
        for e, ref in enumerate((back0, back1, back2)):
            ref[a] = back[(3 * a + e) * MD : (3 * a + e + 1) * MD]


def owner_chunk(half, one, two):
    core, x, y, z = place()
    core = core ^ half
    first = jnp.where(core == 0, y, x)
    second = jnp.where(core == 0, x, z)
    number = core * 16 + ((first + one) & 3) * 4 + ((second + two) & 3)
    return pl.multiple_of(number * 16, 16)


def pack(grads, keep, send):
    for half, ref in enumerate((keep, send)):
        for one in range(4):
            for two in range(4):
                at = owner_chunk(half, one, two)
                for m in range(3):
                    ref[one, two, m] = grads[m, pl.ds(at, 16), :].astype(BF)


def dec_grads(up, own, down, slots, grid, dst, mean, cot, w_dst, keep, send, part_out, grads):
    grads[0] = (
        mm(up[...], slots[0:192], TN) + mm(own[...], slots[192:384], TN) + mm(down[...], slots[384:576], TN)
    )
    grads[1] = mm(grid[...], dst[...], TN)
    grads[2] = mm(mean[...], cot[...], TN)
    pack(grads, keep, send)
    for g in range(0, GD, 256):
        part_out[g : g + 256] = cot[g : g + 256].astype(F32) + mm(dst[g : g + 256], w_dst[...], NT)


def enc_backward(up, own, down, slope, hot, w_src, w_dst, w_out,
                 grad_out, dround_out, dst_out, slots_out, back0, back1, back2, change):
    total = up[...].astype(F32) + own[...].astype(F32) + down[...].astype(F32)
    rounded = total.astype(BF)
    dround_out[...] = rounded
    upstream = mm(rounded, w_out[...], NT)
    received = jnp.zeros((MD, D), F32)
    for k in range(KE):
        value = (upstream * slope[k].astype(F32)).astype(BF)
        change[k * MD : (k + 1) * MD] = value
        received = received + value.astype(F32)
    dst = received.astype(BF)
    dst_out[...] = dst
    for e, ref in enumerate((back0, back1, back2)):
        rows = jnp.concatenate([hot[(3 * a + e) * CAP : (3 * a + e + 1) * CAP] for a in range(3)], axis=0)
        slots = mm(rows, change[...]).astype(BF)
        back = mm(slots, w_src[...], NT).astype(BF)
        for a in range(3):
            i = 3 * a + e
            slots_out[i * CAP : (i + 1) * CAP] = slots[a * CAP : (a + 1) * CAP]
            ref[a] = back[a * CAP : (a + 1) * CAP]
    grad_out[...] = total + mm(dst, w_dst[...], NT)


def enc_grads(recv, slots, latent, dst, mean, dround, keep, send, grads):
    grads[0] = mm(recv[...], slots[...], TN)
    grads[1] = mm(latent[...], dst[...], TN)
    grads[2] = mm(mean[...], dround[...], TN)
    pack(grads, keep, send)


def put_rows(send, up, left, own, right, down, part, out):
    for g in range(0, GD, 256):
        hot = jnp.concatenate(
            [one_hot(send[i : i + 1, :] - g, (256, CAP), 0) for i in range(9)], axis=1
        )
        rows = [up[e] for e in range(3)] + [left[1], own[1], right[1]] + [down[e] for e in range(3)]
        out[g : g + 256] = part[g : g + 256] + mm(hot, jnp.concatenate(rows, axis=0))


def unpack(half, *refs):
    parts, outs, (whole, sems) = refs[:5], refs[-8:-2], refs[-2:]
    rows = [[parts[0].at[t] for t in range(4)], [parts[1].at[t] for t in range(4)],
            [parts[3 + t // 2].at[t % 2] for t in range(4)], [parts[2].at[t] for t in range(4)]]
    start = pl.multiple_of((place()[0] ^ half) * 256, 256)
    copies = [pltpu.make_async_copy(whole.at[m], outs[m].at[pl.ds(start, 256)], sems.at[m]) for m in range(6)]
    for m in range(6):
        for one in range(4):
            for two in range(4):
                at = pl.multiple_of(owner_chunk(half, -one, -two) - start, 16)
                whole[m, pl.ds(at, 16), :] = rows[one][two][m].astype(F32)
        copies[m].start()
    for copy in copies:
        copy.wait()


def pairs(x, partner):
    return lax.ppermute(x, AXES, [(i, partner(i)) for i in range(NB * NM) if partner(i) is not None])


def other_core(x):
    return pairs(x, lambda i: i ^ 1)


def other_chip(x):
    return pairs(x, lambda i: i // NM * NM + (i % NM + (1 if i % 2 else -1)) % NM)


def near_band(x):
    return pairs(x, lambda i: i ^ NM)


def far_band(x):
    def partner(i):
        to = i + (NM if i // NM % 2 else -NM)
        return to if 0 <= to < NB * NM else None

    return pairs(x, partner)


def device(x, y, z, core):
    return (x * 4 + z) * NM + y * 2 + core


def torus_shift(x, stage, by):
    def partner(i):
        b, j = divmod(i, NM)
        at = [b // 4, j // 2, b % 4]
        axis = ((1, 0, 2), (0, 2, 1))[j % 2][stage - 1]
        at[axis] = (at[axis] + by) % 4
        return device(*at, j % 2)

    return pairs(x, partner)


def add(*values):
    total = values[0].astype(F32)
    for v in values[1:]:
        total = total + v.astype(F32)
    return total.astype(BF)


def chip_sum(*packed):
    got = [other_core(send) for _, send in packed]
    return [[add(keep[d], g[d]) for d in range(4)] for (keep, _), g in zip(packed, got)]


def first_step(enc, dec):
    before = torus_shift(enc[2], 1, 1)
    after = torus_shift(dec[2], 1, -1)
    on = jnp.concatenate([add(enc[1], before), dec[1]], axis=1)
    back = jnp.concatenate([enc[3], add(dec[3], after)], axis=1)
    return on, back


def first_sum(enc, dec, on, back):
    on, back = torus_shift(on, 1, 1), torus_shift(back, 1, -1)
    own = jnp.concatenate([enc[0], dec[0]], axis=1)
    return [add(own[d], on[d], back[d]) for d in range(4)]


def second_sum(s):
    got = [torus_shift(s[d], 2, d) for d in (1, 2, 3)]
    return add(s[0], *got)


def stage_three(v):
    one, two, three = (torus_shift(v, 3, d) for d in (1, 2, 3))
    return ((v.astype(F32) + two.astype(F32)) + (one.astype(F32) + three.astype(F32))).astype(BF)


def gather(v, stage):
    return jnp.stack([v] + [torus_shift(v, stage, d) for d in (1, 2, 3)])


def ring_gather(v):
    before, after = torus_shift(v, 1, 1), torus_shift(v, 1, -1)
    return v, before, after, torus_shift(before[:2], 1, 1), torus_shift(after[2:], 1, -1)


def first_exchange(x0, x1, x2):
    return other_chip(x0), x1, other_core(x2)


def second_exchange(left, own, right):
    up = far_band(jnp.stack([left[0], own[0], right[0]]))
    down = near_band(jnp.stack([left[2], own[2], right[2]]))
    return up, down


def body(grid_latent, mesh_latent, w_src_enc, w_dst_enc, w_out_enc, w_src_dec, w_dst_dec, w_out_dec, grid_cot,
         enc_send, enc_slot, enc_count, dec_send, dec_slot, dec_count):
    core, _, _, z = place()
    odd = z & 1
    sends = jnp.concatenate([enc_send, dec_send], axis=0)
    sends = jnp.where(odd == 1, sends[:, ::-1], sends)
    sends = jnp.where(core == 1, sends[:, :, ::-1], sends)
    sends = jnp.pad(sends.reshape(2, 9, CAP), ((0, 0), (0, 7), (0, 0))).reshape(32, CAP)

    block = ((3, ROWS, D), BF)
    one = ((ROWS, D), BF)
    x0, own0, own1, own2, x2 = call(pick_rows, [block, one, one, one, block], "pick_rows", 1300000000)(sends, grid_latent)
    hot_enc, back_enc, target, upstream = call(
        prepare,
        [((KE * MD, 9 * CAP), BF), ((9 * CAP, KE * MD), BF), ((GD, D), F32), ((GD, D), F32)],
        "prepare", 4000000000,
    )(enc_slot.T, grid_latent, grid_cot, w_dst_dec, w_out_dec)
    down = near_band(own2)
    up = far_band(own0)
    left, right = other_chip(x0), other_core(x2)
    down2 = near_band(jnp.stack([left[2], right[2]]))
    up2 = far_band(jnp.stack([left[0], right[0]]))
    mean_enc, slope, mesh_new, table, recv = call(
        enc_forward,
        [((MD, D), BF), ((KE, MD, D), BF), ((MD, D), BF), ((16, CAP), F32), ((9 * CAP, D), BF)],
        "enc_forward", 3400000000, scratch=[pltpu.VMEM((9 * CAP, D), BF)],
    )(up, up2, down, down2, left, right, own1, hot_enc, enc_count.reshape(1, MD), mesh_latent, w_src_enc, w_dst_enc, w_out_enc)

    up = far_band(mesh_new)
    down = near_band(mesh_new)
    hot_dec, back_dec = call(
        merge_index, [((4, KD * STEP, NEAR), BF), ((4, 9 * MD, KD * STEP), BF)], "merge_index", 2000000000
    )(table, dec_slot.T)
    up, down, hot_dec, back_dec = lax.optimization_barrier((up, down, hot_dec, back_dec))
    mine = jnp.stack([up, mesh_new, down])
    left = other_chip(mine)
    right = other_core(mine)
    near = [jnp.concatenate([left[a], mine[a], right[a]], axis=0) for a in range(3)]

    rows = ((GD, D), BF)
    mean_dec, dst_dec, slots_dec, b0, b1, b2 = call(
        decoder,
        [rows, rows, ((9 * MD, D), BF)] + [((3, MD, D), BF)] * 3,
        "decoder", 5500000000,
        scratch=[pltpu.VMEM((NEAR, D), BF), pltpu.VMEM((9 * MD, D), F32)],
    )(*near, hot_dec, back_dec, dec_count.reshape(1, GD), target, upstream, w_src_dec)

    left = other_chip(b0)
    right = other_core(b2)
    sums = [left[a].astype(F32) + b1[a].astype(F32) + right[a].astype(F32) for a in range(3)]
    up = far_band(sums[0].astype(BF))
    down = near_band(sums[2].astype(BF))

    half = ((4, 4, 3, 16, D), BF)
    *packed_dec, grid_part = call(
        dec_grads, [half, half, ((GD, D), F32)], "dec_grads", 2300000000, scratch=[pltpu.VMEM((3, D, D), F32)],
    )(*near, slots_dec, grid_latent, dst_dec, mean_dec, grid_cot, w_dst_dec)

    mesh_grad, dround, dst_enc, slots_enc, x0, x1, x2 = call(
        enc_backward,
        [((MD, D), F32), ((MD, D), BF), ((MD, D), BF), ((9 * CAP, D), BF)] + [((3, CAP, D), BF)] * 3,
        "enc_backward", 3200000000, scratch=[pltpu.VMEM((KE * MD, D), BF)],
    )(up, sums[1], down, slope, back_enc, w_src_enc, w_dst_enc, w_out_enc)
    packed_enc = call(
        enc_grads, [half, half], "enc_grads", 700000000, scratch=[pltpu.VMEM((3, D, D), F32)],
    )(recv, slots_enc, mesh_latent, dst_enc, mean_enc, dround)

    left, _, right = first_exchange(x0, x1, x2)
    enc, dec = chip_sum(packed_enc, packed_dec)
    on, back = first_step(enc, dec)
    on, back, left, right = lax.optimization_barrier((on, back, left, right))
    up, down = second_exchange(left, x1, right)
    part_sums = first_sum(enc, dec, on, back)
    part_sum = second_sum(part_sums)
    (grid_grad,) = call(put_rows, [((GD, D), F32)], "put_rows", 1300000000)(
        sends, up, left, x1, right, down, grid_part
    )
    v = gather(stage_three(part_sum), 2)
    v, grid_grad = lax.optimization_barrier((v, grid_grad))
    parts = ring_gather(v)
    others = [other_core(part) for part in parts]
    square = ((D, D), F32)
    anywhere = pl.BlockSpec(memory_space=pl.ANY)
    unpacker = functools.partial(
        call, outs=[square] * 6, flops=50000000,
        scratch=[pltpu.VMEM((6, 256, D), F32), pltpu.SemaphoreType.DMA((6,))], out_specs=[anywhere] * 6,
    )
    grads = unpacker(functools.partial(unpack, 0), name="unpack_own")(*parts)
    grads = unpacker(
        functools.partial(unpack, 1), name="unpack_other",
        in_specs=[pl.BlockSpec(memory_space=pltpu.VMEM)] * 5 + [anywhere] * 6,
        input_output_aliases={m + 5: m for m in range(6)},
    )(*others, *grads)
    return (grid_grad, mesh_grad, *grads)


def solution(mesh):
    rows = P(AXES, None)
    whole = P()
    return jax.shard_map(
        body,
        mesh=mesh,
        in_specs=(rows, rows) + (whole,) * 6 + (rows, P(AXES, None, None, None), rows, P(AXES),
                                               P(AXES, None, None, None), rows, P(AXES)),
        out_specs=(rows, rows) + (whole,) * 6,
        check_vma=False,
    )
```

```python
import jax
import jax.numpy as jnp
from jax import lax
from jax.experimental import pallas as pl
from jax.experimental.pallas import tpu as pltpu
from jax.sharding import PartitionSpec as P

D = 512
GD = 1024
MD = 64
KE = 32
KD = 3
CAP = 128
ROWS = CAP + 16
NEAR = 640
STEP = 256
NB = 16
NM = 8
AXES = ("band", "mesh")
BF = jnp.bfloat16
F32 = jnp.float32
MIB = 1 << 20

NN = (((1,), (0,)), ((), ()))
NT = (((1,), (1,)), ((), ()))
TN = (((0,), (0,)), ((), ()))


def mm(a, b, dims=NN):
    return lax.dot_general(a, b, dims, preferred_element_type=F32)


def iota(shape, dim):
    return lax.broadcasted_iota(jnp.int32, shape, dim)


def one_hot(index, shape, dim):
    return jnp.where(iota(shape, dim) == index, 1.0, 0.0).astype(BF)


def place():
    b, j = lax.axis_index("band"), lax.axis_index("mesh")
    return j & 1, b >> 2, j >> 1, b & 3


def own_number(block):
    core, _, _, z = place()
    odd = z & 1
    a = (block * 11) >> 5
    e = block - 3 * a
    return 3 * jnp.where(odd == 1, 2 - a, a) + jnp.where(core == 1, 2 - e, e)


def own_slot(slot):
    return (own_number(slot >> 7) << 7) | (slot & 127)


def call(body, outs, name, flops, scratch=(), vmem=16, **kwargs):
    return pl.pallas_call(
        body,
        out_shape=[jax.ShapeDtypeStruct(s, t) for s, t in outs],
        scratch_shapes=list(scratch),
        name=name,
        cost_estimate=pl.CostEstimate(flops=flops, bytes_accessed=4 * MIB, transcendentals=0),
        compiler_params=pltpu.CompilerParams(vmem_limit_bytes=vmem * MIB),
        **kwargs,
    )


def pick_rows(send_ref, latent_ref, left, own0, own1, own2, right):
    columns = send_ref[0:16].T
    table = send_ref[16:32].astype(F32)
    pad = jnp.zeros((16, D - CAP), BF)
    for e in range(3):
        hot = jnp.concatenate(
            [one_hot(columns[:, 3 * a + e : 3 * a + e + 1], (CAP, GD), 1) for a in range(3)], axis=0
        )
        rows = mm(hot, latent_ref[...]).astype(BF)
        for a in range(3):
            i = 3 * a + e
            out = (left.at[a], (own0, own1, own2)[a], right.at[a])[e]
            out[0:CAP, :] = rows[a * CAP : (a + 1) * CAP]
            numbers = jnp.where(iota((16, CAP), 0) == 0, table[i : i + 1, :], 0.0).astype(BF)
            out[CAP:ROWS, :] = jnp.concatenate([numbers, pad], axis=1)


def sigmoid(v):
    return 0.5 * jnp.tanh(0.5 * v) + 0.5


def prepare(slot, grid, cot, w_dst, w_out, hot_out, back_out, target_out, up_out):
    own = own_slot(slot[...])
    columns = own.T
    for k in range(KE):
        hot_out[k * MD : (k + 1) * MD] = one_hot(columns[:, k : k + 1], (MD, 9 * CAP), 1)
    for k in range(0, KE, 2):
        line = jnp.concatenate([own[k : k + 1], own[k + 1 : k + 2]], axis=1)
        back_out[:, k * MD : (k + 2) * MD] = one_hot(line, (9 * CAP, 2 * MD), 0)
    for g in range(0, GD, 256):
        target_out[g : g + 256] = mm(grid[g : g + 256], w_dst[...])
        up_out[g : g + 256] = mm(cot[g : g + 256], w_out[...], NT)


def enc_forward(up, up2, down, down2, left, right, own, hot, count, latent, w_src, w_dst, w_out,
                mean_out, slope_out, new_out, table_out, recv_out, proj):
    blocks = (up2.at[0], up, up2.at[1], left.at[1], own, right.at[1], down2.at[0], down, down2.at[1])
    for i, block in enumerate(blocks):
        recv_out[i * CAP : (i + 1) * CAP] = block[0:CAP]
        table_out[i : i + 1] = block[CAP:ROWS, 0:CAP].astype(F32)[0:1]
    table_out[9:16] = jnp.zeros((7, CAP), F32)
    for a in range(3):
        part = slice(a * 384, (a + 1) * 384)
        proj[part] = mm(recv_out[part], w_src[...]).astype(BF)
    counts = jnp.broadcast_to(count[...], (8, MD)).T[:, 0:1]
    inverse = 1.0 / counts.astype(F32)
    target = mm(latent[...], w_dst[...])
    total = jnp.zeros((MD, D), F32)
    for c in range(4):
        values = mm(hot[c * 8 * MD : (c + 1) * 8 * MD], proj[...])
        for j in range(8):
            k = 8 * c + j
            pre = values[j * MD : (j + 1) * MD] + target
            weight = jnp.where(k < counts, inverse, 0.0)
            sig = sigmoid(pre)
            act = pre * sig
            total = total + act * weight
            slope_out[k] = ((sig + act * (1.0 - sig)) * weight).astype(BF)
    mean = total.astype(BF)
    mean_out[...] = mean
    new_out[...] = (latent[...].astype(F32) + mm(mean, w_out[...])).astype(BF)


def merge_index(table, slot, hot_out, back_out):
    numbers = table[...].astype(BF)
    for k in range(KD):
        s = slot[k : k + 1, :]
        high, low = own_number(s >> 7), s & 127
        found = mm(numbers, one_hot(low, (CAP, GD), 0))
        value = jnp.sum(jnp.where(iota((16, GD), 0) == high, found, 0.0), axis=0, keepdims=True)
        row = high * MD + value.astype(jnp.int32)
        column = jnp.broadcast_to(row, (8, GD)).T[:, 0:1]
        for c in range(4):
            part = slice(c * STEP, (c + 1) * STEP)
            hot_out[c, k * STEP : (k + 1) * STEP] = one_hot(column[part], (STEP, NEAR), 1)
            back_out[c, :, k * STEP : (k + 1) * STEP] = one_hot(row[:, part], (9 * MD, STEP), 0)


def decoder(up, own, down, hot, back_hot, count, target, upstream, w_src,
            mean_out, dst_out, slots_out, back0, back1, back2, proj, acc):
    proj[0:192] = mm(up[...], w_src[...]).astype(BF)
    proj[192:384] = mm(own[...], w_src[...]).astype(BF)
    proj[384:576] = mm(down[...], w_src[...]).astype(BF)
    proj[576:NEAR] = jnp.zeros((NEAR - 576, D), BF)
    for c in range(4):
        part = slice(c * STEP, (c + 1) * STEP)
        counts = jnp.broadcast_to(count[:, part], (8, STEP)).T[:, 0:1]
        inverse = 1.0 / counts.astype(F32)
        total = jnp.zeros((STEP, D), F32)
        received = jnp.zeros((STEP, D), F32)
        parts = []
        values = mm(hot[c], proj[...])
        for k in range(KD):
            pre = values[k * STEP : (k + 1) * STEP] + target[part]
            weight = jnp.where(k < counts, inverse, 0.0)
            sig = sigmoid(pre)
            act = pre * sig
            total = total + act * weight
            change = (upstream[part] * weight * (sig + act * (1.0 - sig))).astype(BF)
            received = received + change.astype(F32)
            parts.append(change)
        mean_out[part] = total.astype(BF)
        dst_out[part] = received.astype(BF)
        added = mm(back_hot[c], jnp.concatenate(parts, axis=0))
        if c == 0:
            acc[...] = added
        else:
            acc[...] += added
    slots = acc[...].astype(BF)
    slots_out[...] = slots
    back = mm(slots, w_src[...], NT).astype(BF)
    for a in range(3):
        for e, ref in enumerate((back0, back1, back2)):
            ref[a] = back[(3 * a + e) * MD : (3 * a + e + 1) * MD]


def owner_chunk(half, one, two):
    core, x, y, z = place()
    core = core ^ half
    first = jnp.where(core == 0, y, x)
    second = jnp.where(core == 0, x, z)
    number = core * 16 + ((first + one) & 3) * 4 + ((second + two) & 3)
    return pl.multiple_of(number * 16, 16)


def pack(grads, keep, send):
    for half, ref in enumerate((keep, send)):
        for one in range(4):
            for two in range(4):
                at = owner_chunk(half, one, two)
                for m in range(3):
                    ref[one, two, m] = grads[m, pl.ds(at, 16), :].astype(BF)


def dec_grads(up, own, down, slots, grid, dst, mean, cot, w_dst, keep, send, part_out, grads):
    grads[0] = (
        mm(up[...], slots[0:192], TN) + mm(own[...], slots[192:384], TN) + mm(down[...], slots[384:576], TN)
    )
    grads[1] = mm(grid[...], dst[...], TN)
    grads[2] = mm(mean[...], cot[...], TN)
    pack(grads, keep, send)
    for g in range(0, GD, 256):
        part_out[g : g + 256] = cot[g : g + 256].astype(F32) + mm(dst[g : g + 256], w_dst[...], NT)


def enc_backward(up, own, down, slope, hot, w_src, w_dst, w_out,
                 grad_out, dround_out, dst_out, slots_out, back0, back1, back2, change):
    total = up[...].astype(F32) + own[...].astype(F32) + down[...].astype(F32)
    rounded = total.astype(BF)
    dround_out[...] = rounded
    upstream = mm(rounded, w_out[...], NT)
    received = jnp.zeros((MD, D), F32)
    for k in range(KE):
        value = (upstream * slope[k].astype(F32)).astype(BF)
        change[k * MD : (k + 1) * MD] = value
        received = received + value.astype(F32)
    dst = received.astype(BF)
    dst_out[...] = dst
    for e, ref in enumerate((back0, back1, back2)):
        rows = jnp.concatenate([hot[(3 * a + e) * CAP : (3 * a + e + 1) * CAP] for a in range(3)], axis=0)
        slots = mm(rows, change[...]).astype(BF)
        back = mm(slots, w_src[...], NT).astype(BF)
        for a in range(3):
            i = 3 * a + e
            slots_out[i * CAP : (i + 1) * CAP] = slots[a * CAP : (a + 1) * CAP]
            ref[a] = back[a * CAP : (a + 1) * CAP]
    grad_out[...] = total + mm(dst, w_dst[...], NT)


def enc_grads(recv, slots, latent, dst, mean, dround, keep, send, grads):
    grads[0] = mm(recv[...], slots[...], TN)
    grads[1] = mm(latent[...], dst[...], TN)
    grads[2] = mm(mean[...], dround[...], TN)
    pack(grads, keep, send)


def put_rows(send, up, left, own, right, down, part, out):
    for g in range(0, GD, 256):
        hot = jnp.concatenate(
            [one_hot(send[i : i + 1, :] - g, (256, CAP), 0) for i in range(9)], axis=1
        )
        rows = [up[e] for e in range(3)] + [left[1], own[1], right[1]] + [down[e] for e in range(3)]
        out[g : g + 256] = part[g : g + 256] + mm(hot, jnp.concatenate(rows, axis=0))


def unpack(mine, other, *refs):
    outs, (whole, sems) = refs[:6], refs[6:]
    copies = [pltpu.make_async_copy(whole.at[m], outs[m], sems.at[m]) for m in range(6)]
    for m in range(6):
        for half, ref in enumerate((mine, other)):
            for one in range(4):
                for two in range(4):
                    whole[m, pl.ds(owner_chunk(half, -one, -two), 16), :] = ref[one, two, m].astype(F32)
        copies[m].start()
    for copy in copies:
        copy.wait()


def pairs(x, partner):
    return lax.ppermute(x, AXES, [(i, partner(i)) for i in range(NB * NM) if partner(i) is not None])


def other_core(x):
    return pairs(x, lambda i: i ^ 1)


def other_chip(x):
    return pairs(x, lambda i: i // NM * NM + (i % NM + (1 if i % 2 else -1)) % NM)


def near_band(x):
    return pairs(x, lambda i: i ^ NM)


def far_band(x):
    def partner(i):
        to = i + (NM if i // NM % 2 else -NM)
        return to if 0 <= to < NB * NM else None

    return pairs(x, partner)


def device(x, y, z, core):
    return (x * 4 + z) * NM + y * 2 + core


def torus_shift(x, stage, by):
    def partner(i):
        b, j = divmod(i, NM)
        at = [b // 4, j // 2, b % 4]
        axis = ((1, 0, 2), (0, 2, 1))[j % 2][stage - 1]
        at[axis] = (at[axis] + by) % 4
        return device(*at, j % 2)

    return pairs(x, partner)


def add(*values):
    total = values[0].astype(F32)
    for v in values[1:]:
        total = total + v.astype(F32)
    return total.astype(BF)


def chip_sum(*packed):
    got = [other_core(send) for _, send in packed]
    return [[add(keep[d], g[d]) for d in range(4)] for (keep, _), g in zip(packed, got)]


def first_step(enc, dec):
    before = torus_shift(enc[2], 1, 1)
    after = torus_shift(dec[2], 1, -1)
    on = jnp.concatenate([add(enc[1], before), dec[1]], axis=1)
    back = jnp.concatenate([enc[3], add(dec[3], after)], axis=1)
    return on, back


def first_sum(enc, dec, on, back):
    on, back = torus_shift(on, 1, 1), torus_shift(back, 1, -1)
    own = jnp.concatenate([enc[0], dec[0]], axis=1)
    return [add(own[d], on[d], back[d]) for d in range(4)]


def second_sum(s):
    got = [torus_shift(s[d], 2, d) for d in (1, 2, 3)]
    return add(s[0], *got)


def stage_three(v):
    one, two, three = (torus_shift(v, 3, d) for d in (1, 2, 3))
    return ((v.astype(F32) + two.astype(F32)) + (one.astype(F32) + three.astype(F32))).astype(BF)


def gather(v, stage):
    return jnp.stack([v] + [torus_shift(v, stage, d) for d in (1, 2, 3)])


def ring_gather(v):
    before, after = torus_shift(v, 1, 1), torus_shift(v, 1, -1)
    across = jnp.concatenate([torus_shift(before[:2], 1, 1), torus_shift(after[2:], 1, -1)], axis=0)
    return jnp.stack([v, before, across, after])


def first_exchange(x0, x1, x2):
    return other_chip(x0), x1, other_core(x2)


def second_exchange(left, own, right):
    up = far_band(jnp.stack([left[0], own[0], right[0]]))
    down = near_band(jnp.stack([left[2], own[2], right[2]]))
    return up, down


def body(grid_latent, mesh_latent, w_src_enc, w_dst_enc, w_out_enc, w_src_dec, w_dst_dec, w_out_dec, grid_cot,
         enc_send, enc_slot, enc_count, dec_send, dec_slot, dec_count):
    core, _, _, z = place()
    odd = z & 1
    sends = jnp.concatenate([enc_send, dec_send], axis=0)
    sends = jnp.where(odd == 1, sends[:, ::-1], sends)
    sends = jnp.where(core == 1, sends[:, :, ::-1], sends)
    sends = jnp.pad(sends.reshape(2, 9, CAP), ((0, 0), (0, 7), (0, 0))).reshape(32, CAP)

    block = ((3, ROWS, D), BF)
    one = ((ROWS, D), BF)
    x0, own0, own1, own2, x2 = call(pick_rows, [block, one, one, one, block], "pick_rows", 1300000000)(sends, grid_latent)
    hot_enc, back_enc, target, upstream = call(
        prepare,
        [((KE * MD, 9 * CAP), BF), ((9 * CAP, KE * MD), BF), ((GD, D), F32), ((GD, D), F32)],
        "prepare", 4000000000,
    )(enc_slot.T, grid_latent, grid_cot, w_dst_dec, w_out_dec)
    down = near_band(own2)
    up = far_band(own0)
    left, right = other_chip(x0), other_core(x2)
    down2 = near_band(jnp.stack([left[2], right[2]]))
    up2 = far_band(jnp.stack([left[0], right[0]]))
    mean_enc, slope, mesh_new, table, recv = call(
        enc_forward,
        [((MD, D), BF), ((KE, MD, D), BF), ((MD, D), BF), ((16, CAP), F32), ((9 * CAP, D), BF)],
        "enc_forward", 3400000000, scratch=[pltpu.VMEM((9 * CAP, D), BF)],
    )(up, up2, down, down2, left, right, own1, hot_enc, enc_count.reshape(1, MD), mesh_latent, w_src_enc, w_dst_enc, w_out_enc)

    up = far_band(mesh_new)
    down = near_band(mesh_new)
    hot_dec, back_dec = call(
        merge_index, [((4, KD * STEP, NEAR), BF), ((4, 9 * MD, KD * STEP), BF)], "merge_index", 2000000000
    )(table, dec_slot.T)
    up, down, hot_dec, back_dec = lax.optimization_barrier((up, down, hot_dec, back_dec))
    mine = jnp.stack([up, mesh_new, down])
    left = other_chip(mine)
    right = other_core(mine)
    near = [jnp.concatenate([left[a], mine[a], right[a]], axis=0) for a in range(3)]

    rows = ((GD, D), BF)
    mean_dec, dst_dec, slots_dec, b0, b1, b2 = call(
        decoder,
        [rows, rows, ((9 * MD, D), BF)] + [((3, MD, D), BF)] * 3,
        "decoder", 5500000000,
        scratch=[pltpu.VMEM((NEAR, D), BF), pltpu.VMEM((9 * MD, D), F32)],
    )(*near, hot_dec, back_dec, dec_count.reshape(1, GD), target, upstream, w_src_dec)

    left = other_chip(b0)
    right = other_core(b2)
    sums = [left[a].astype(F32) + b1[a].astype(F32) + right[a].astype(F32) for a in range(3)]
    up = far_band(sums[0].astype(BF))
    down = near_band(sums[2].astype(BF))

    half = ((4, 4, 3, 16, D), BF)
    *packed_dec, grid_part = call(
        dec_grads, [half, half, ((GD, D), F32)], "dec_grads", 2300000000, scratch=[pltpu.VMEM((3, D, D), F32)],
    )(*near, slots_dec, grid_latent, dst_dec, mean_dec, grid_cot, w_dst_dec)

    mesh_grad, dround, dst_enc, slots_enc, x0, x1, x2 = call(
        enc_backward,
        [((MD, D), F32), ((MD, D), BF), ((MD, D), BF), ((9 * CAP, D), BF)] + [((3, CAP, D), BF)] * 3,
        "enc_backward", 3200000000, scratch=[pltpu.VMEM((KE * MD, D), BF)],
    )(up, sums[1], down, slope, back_enc, w_src_enc, w_dst_enc, w_out_enc)
    packed_enc = call(
        enc_grads, [half, half], "enc_grads", 700000000, scratch=[pltpu.VMEM((3, D, D), F32)],
    )(recv, slots_enc, mesh_latent, dst_enc, mean_enc, dround)

    left, _, right = first_exchange(x0, x1, x2)
    enc, dec = chip_sum(packed_enc, packed_dec)
    on, back = first_step(enc, dec)
    on, back, left, right = lax.optimization_barrier((on, back, left, right))
    up, down = second_exchange(left, x1, right)
    part_sums = first_sum(enc, dec, on, back)
    part_sum = second_sum(part_sums)
    (grid_grad,) = call(put_rows, [((GD, D), F32)], "put_rows", 1300000000)(
        sends, up, left, x1, right, down, grid_part
    )
    v = gather(stage_three(part_sum), 2)
    v, grid_grad = lax.optimization_barrier((v, grid_grad))
    v = ring_gather(v)
    grads = call(
        unpack, [((D, D), F32)] * 6, "unpack", 100000000,
        scratch=[pltpu.VMEM((6, D, D), F32), pltpu.SemaphoreType.DMA((6,))],
        out_specs=[pl.BlockSpec(memory_space=pl.ANY)] * 6,
    )(v, other_core(v))
    return (grid_grad, mesh_grad, *grads)


def solution(mesh):
    rows = P(AXES, None)
    whole = P()
    return jax.shard_map(
        body,
        mesh=mesh,
        in_specs=(rows, rows) + (whole,) * 6 + (rows, P(AXES, None, None, None), rows, P(AXES),
                                               P(AXES, None, None, None), rows, P(AXES)),
        out_specs=(rows, rows) + (whole,) * 6,
        check_vma=False,
    )
```

```python
import functools

import jax
import jax.numpy as jnp
from jax import lax
from jax.experimental import pallas as pl
from jax.experimental.pallas import tpu as pltpu
from jax.sharding import PartitionSpec as P

D = 512
GD = 1024
MD = 64
KE = 32
KD = 3
CAP = 128
ROWS = CAP + 16
NEAR = 640
STEP = 256
NB = 16
NM = 8
AXES = ("band", "mesh")
BF = jnp.bfloat16
F32 = jnp.float32
MIB = 1 << 20

NN = (((1,), (0,)), ((), ()))
NT = (((1,), (1,)), ((), ()))
TN = (((0,), (0,)), ((), ()))


def mm(a, b, dims=NN):
    return lax.dot_general(a, b, dims, preferred_element_type=F32)


def iota(shape, dim):
    return lax.broadcasted_iota(jnp.int32, shape, dim)


def one_hot(index, shape, dim):
    return jnp.where(iota(shape, dim) == index, 1.0, 0.0).astype(BF)


def place():
    b, j = lax.axis_index("band"), lax.axis_index("mesh")
    return j & 1, b >> 2, j >> 1, b & 3


def own_number(block):
    core, _, _, z = place()
    odd = z & 1
    a = (block * 11) >> 5
    e = block - 3 * a
    return 3 * jnp.where(odd == 1, 2 - a, a) + jnp.where(core == 1, 2 - e, e)


def own_slot(slot):
    return (own_number(slot >> 7) << 7) | (slot & 127)


def call(body, outs, name, flops, scratch=(), vmem=16, **kwargs):
    return pl.pallas_call(
        body,
        out_shape=[jax.ShapeDtypeStruct(s, t) for s, t in outs],
        scratch_shapes=list(scratch),
        name=name,
        cost_estimate=pl.CostEstimate(flops=flops, bytes_accessed=4 * MIB, transcendentals=0),
        compiler_params=pltpu.CompilerParams(vmem_limit_bytes=vmem * MIB),
        **kwargs,
    )


def pick_rows(send_ref, latent_ref, left, own0, own1, own2, right):
    columns = send_ref[0:16].T
    table = send_ref[16:32].astype(F32)
    pad = jnp.zeros((16, D - CAP), BF)
    for e in range(3):
        hot = jnp.concatenate(
            [one_hot(columns[:, 3 * a + e : 3 * a + e + 1], (CAP, GD), 1) for a in range(3)], axis=0
        )
        rows = mm(hot, latent_ref[...]).astype(BF)
        for a in range(3):
            i = 3 * a + e
            out = (left.at[a], (own0, own1, own2)[a], right.at[a])[e]
            out[0:CAP, :] = rows[a * CAP : (a + 1) * CAP]
            numbers = jnp.where(iota((16, CAP), 0) == 0, table[i : i + 1, :], 0.0).astype(BF)
            out[CAP:ROWS, :] = jnp.concatenate([numbers, pad], axis=1)


def sigmoid(v):
    return 0.5 * jnp.tanh(0.5 * v) + 0.5


def prepare(slot, grid, cot, w_dst, w_out, hot_out, back_out, target_out, up_out):
    own = own_slot(slot[...])
    columns = own.T
    for k in range(KE):
        hot_out[k * MD : (k + 1) * MD] = one_hot(columns[:, k : k + 1], (MD, 9 * CAP), 1)
    for k in range(0, KE, 2):
        line = jnp.concatenate([own[k : k + 1], own[k + 1 : k + 2]], axis=1)
        back_out[:, k * MD : (k + 2) * MD] = one_hot(line, (9 * CAP, 2 * MD), 0)

    def products(c, _):
        part = pl.ds(pl.multiple_of(c * STEP, STEP), STEP)
        target_out[part] = mm(grid[part], w_dst[...])
        up_out[part] = mm(cot[part], w_out[...], NT)
        return 0

    lax.fori_loop(0, 4, products, 0)


def enc_forward(up, up2, down, down2, left, right, own, hot, count, latent, w_src, w_dst, w_out,
                mean_out, slope_out, new_out, table_out, recv_out, proj):
    blocks = (up2.at[0], up, up2.at[1], left.at[1], own, right.at[1], down2.at[0], down, down2.at[1])
    for i, block in enumerate(blocks):
        recv_out[i * CAP : (i + 1) * CAP] = block[0:CAP]
        table_out[i : i + 1] = block[CAP:ROWS, 0:CAP].astype(F32)[0:1]
    table_out[9:16] = jnp.zeros((7, CAP), F32)
    for a in range(3):
        part = slice(a * 384, (a + 1) * 384)
        proj[part] = mm(recv_out[part], w_src[...]).astype(BF)
    counts = jnp.broadcast_to(count[...], (8, MD)).T[:, 0:1]
    inverse = 1.0 / counts.astype(F32)
    target = mm(latent[...], w_dst[...])
    total = jnp.zeros((MD, D), F32)
    for c in range(4):
        values = mm(hot[c * 8 * MD : (c + 1) * 8 * MD], proj[...])
        for j in range(8):
            k = 8 * c + j
            pre = values[j * MD : (j + 1) * MD] + target
            weight = jnp.where(k < counts, inverse, 0.0)
            sig = sigmoid(pre)
            act = pre * sig
            total = total + act * weight
            slope_out[k] = ((sig + act * (1.0 - sig)) * weight).astype(BF)
    mean = total.astype(BF)
    mean_out[...] = mean
    new_out[...] = (latent[...].astype(F32) + mm(mean, w_out[...])).astype(BF)


def merge_index(table, slot, hot_out, back_out):
    numbers = table[...].astype(BF)
    for k in range(KD):
        s = slot[k : k + 1, :]
        high, low = own_number(s >> 7), s & 127
        found = mm(numbers, one_hot(low, (CAP, GD), 0))
        value = jnp.sum(jnp.where(iota((16, GD), 0) == high, found, 0.0), axis=0, keepdims=True)
        row = high * MD + value.astype(jnp.int32)
        column = jnp.broadcast_to(row, (8, GD)).T[:, 0:1]
        for c in range(4):
            part = slice(c * STEP, (c + 1) * STEP)
            hot_out[c, k * STEP : (k + 1) * STEP] = one_hot(column[part], (STEP, NEAR), 1)
            back_out[c, :, k * STEP : (k + 1) * STEP] = one_hot(row[:, part], (9 * MD, STEP), 0)


def decoder(up, own, down, hot, back_hot, count, target, upstream, w_src,
            mean_out, dst_out, slots_out, back0, back1, back2, proj, acc):
    proj[0:192] = mm(up[...], w_src[...]).astype(BF)
    proj[192:384] = mm(own[...], w_src[...]).astype(BF)
    proj[384:576] = mm(down[...], w_src[...]).astype(BF)
    proj[576:NEAR] = jnp.zeros((NEAR - 576, D), BF)
    acc[...] = jnp.zeros((9 * MD, D), F32)

    def quarter(c, _):
        part = pl.ds(pl.multiple_of(c * STEP, STEP), STEP)
        counts = jnp.broadcast_to(count[:, part], (8, STEP)).T[:, 0:1]
        inverse = 1.0 / counts.astype(F32)
        total = jnp.zeros((STEP, D), F32)
        received = jnp.zeros((STEP, D), F32)
        parts = []
        values = mm(hot[c], proj[...])
        for k in range(KD):
            pre = values[k * STEP : (k + 1) * STEP] + target[part]
            weight = jnp.where(k < counts, inverse, 0.0)
            sig = sigmoid(pre)
            act = pre * sig
            total = total + act * weight
            change = (upstream[part] * weight * (sig + act * (1.0 - sig))).astype(BF)
            received = received + change.astype(F32)
            parts.append(change)
        mean_out[part] = total.astype(BF)
        dst_out[part] = received.astype(BF)
        acc[...] += mm(back_hot[c], jnp.concatenate(parts, axis=0))
        return 0

    lax.fori_loop(0, 4, quarter, 0)
    slots = acc[...].astype(BF)
    slots_out[...] = slots
    back = mm(slots, w_src[...], NT).astype(BF)
    for a in range(3):
        for e, ref in enumerate((back0, back1, back2)):
            ref[a] = back[(3 * a + e) * MD : (3 * a + e + 1) * MD]


def owner_chunk(half, one, two):
    core, x, y, z = place()
    core = core ^ half
    first = jnp.where(core == 0, y, x)
    second = jnp.where(core == 0, x, z)
    number = core * 16 + ((first + one) & 3) * 4 + ((second + two) & 3)
    return pl.multiple_of(number * 16, 16)


def pack(grads, keep, send):
    for half, ref in enumerate((keep, send)):

        def chunk(i, _, half=half, ref=ref):
            at = owner_chunk(half, i >> 2, i & 3)
            for m in range(3):
                ref[i >> 2, i & 3, m] = grads[m, pl.ds(at, 16), :].astype(BF)
            return 0

        lax.fori_loop(0, 16, chunk, 0)


def dec_grads(up, own, down, slots, grid, dst, mean, cot, w_dst, keep, send, part_out, grads):
    grads[0] = (
        mm(up[...], slots[0:192], TN) + mm(own[...], slots[192:384], TN) + mm(down[...], slots[384:576], TN)
    )
    grads[1] = mm(grid[...], dst[...], TN)
    grads[2] = mm(mean[...], cot[...], TN)
    pack(grads, keep, send)

    def direct(c, _):
        part = pl.ds(pl.multiple_of(c * STEP, STEP), STEP)
        part_out[part] = cot[part].astype(F32) + mm(dst[part], w_dst[...], NT)
        return 0

    lax.fori_loop(0, 4, direct, 0)


def enc_backward(up, own, down, slope, hot, w_src, w_dst, w_out,
                 grad_out, dround_out, dst_out, slots_out, back0, back1, back2, change):
    total = up[...].astype(F32) + own[...].astype(F32) + down[...].astype(F32)
    rounded = total.astype(BF)
    dround_out[...] = rounded
    upstream = mm(rounded, w_out[...], NT)
    received = jnp.zeros((MD, D), F32)
    for k in range(KE):
        value = (upstream * slope[k].astype(F32)).astype(BF)
        change[k * MD : (k + 1) * MD] = value
        received = received + value.astype(F32)
    dst = received.astype(BF)
    dst_out[...] = dst
    for e, ref in enumerate((back0, back1, back2)):
        rows = jnp.concatenate([hot[(3 * a + e) * CAP : (3 * a + e + 1) * CAP] for a in range(3)], axis=0)
        slots = mm(rows, change[...]).astype(BF)
        back = mm(slots, w_src[...], NT).astype(BF)
        for a in range(3):
            i = 3 * a + e
            slots_out[i * CAP : (i + 1) * CAP] = slots[a * CAP : (a + 1) * CAP]
            ref[a] = back[a * CAP : (a + 1) * CAP]
    grad_out[...] = total + mm(dst, w_dst[...], NT)


def enc_grads(recv, slots, latent, dst, mean, dround, keep, send, grads):
    grads[0] = mm(recv[...], slots[...], TN)
    grads[1] = mm(latent[...], dst[...], TN)
    grads[2] = mm(mean[...], dround[...], TN)
    pack(grads, keep, send)


def put_rows(send, up, left, own, right, down, part, out):
    def quarter(c, _):
        hot = jnp.concatenate(
            [one_hot(send[i : i + 1, :] - c * STEP, (STEP, CAP), 0) for i in range(9)], axis=1
        )
        rows = [up[e] for e in range(3)] + [left[1], own[1], right[1]] + [down[e] for e in range(3)]
        at = pl.ds(pl.multiple_of(c * STEP, STEP), STEP)
        out[at] = part[at] + mm(hot, jnp.concatenate(rows, axis=0))
        return 0

    lax.fori_loop(0, 4, quarter, 0)


def unpack(half, *refs):
    parts, outs, (whole, sems) = refs[:5], refs[-8:-2], refs[-2:]
    rows = [[parts[0].at[t] for t in range(4)], [parts[1].at[t] for t in range(4)],
            [parts[3 + t // 2].at[t % 2] for t in range(4)], [parts[2].at[t] for t in range(4)]]
    start = pl.multiple_of((place()[0] ^ half) * 256, 256)
    copies = [pltpu.make_async_copy(whole.at[m], outs[m].at[pl.ds(start, 256)], sems.at[m]) for m in range(6)]
    for m in range(6):
        for one in range(4):
            for two in range(4):
                at = pl.multiple_of(owner_chunk(half, -one, -two) - start, 16)
                whole[m, pl.ds(at, 16), :] = rows[one][two][m].astype(F32)
        copies[m].start()
    for copy in copies:
        copy.wait()


def pairs(x, partner):
    return lax.ppermute(x, AXES, [(i, partner(i)) for i in range(NB * NM) if partner(i) is not None])


def other_core(x):
    return pairs(x, lambda i: i ^ 1)


def other_chip(x):
    return pairs(x, lambda i: i // NM * NM + (i % NM + (1 if i % 2 else -1)) % NM)


def near_band(x):
    return pairs(x, lambda i: i ^ NM)


def far_band(x):
    def partner(i):
        to = i + (NM if i // NM % 2 else -NM)
        return to if 0 <= to < NB * NM else None

    return pairs(x, partner)


def device(x, y, z, core):
    return (x * 4 + z) * NM + y * 2 + core


def torus_shift(x, stage, by):
    def partner(i):
        b, j = divmod(i, NM)
        at = [b // 4, j // 2, b % 4]
        axis = ((1, 0, 2), (0, 2, 1))[j % 2][stage - 1]
        at[axis] = (at[axis] + by) % 4
        return device(*at, j % 2)

    return pairs(x, partner)


def add(*values):
    total = values[0].astype(F32)
    for v in values[1:]:
        total = total + v.astype(F32)
    return total.astype(BF)


def chip_sum(*packed):
    got = [other_core(send) for _, send in packed]
    return [[add(keep[d], g[d]) for d in range(4)] for (keep, _), g in zip(packed, got)]


def first_step(enc, dec):
    before = torus_shift(enc[2], 1, 1)
    after = torus_shift(dec[2], 1, -1)
    on = jnp.concatenate([add(enc[1], before), dec[1]], axis=1)
    back = jnp.concatenate([enc[3], add(dec[3], after)], axis=1)
    return on, back


def first_sum(enc, dec, on, back):
    on, back = torus_shift(on, 1, 1), torus_shift(back, 1, -1)
    own = jnp.concatenate([enc[0], dec[0]], axis=1)
    return [add(own[d], on[d], back[d]) for d in range(4)]


def second_sum(s):
    got = [torus_shift(s[d], 2, d) for d in (1, 2, 3)]
    return add(s[0], *got)


def stage_three(v):
    one, two, three = (torus_shift(v, 3, d) for d in (1, 2, 3))
    return ((v.astype(F32) + two.astype(F32)) + (one.astype(F32) + three.astype(F32))).astype(BF)


def gather(v, stage):
    return jnp.stack([v] + [torus_shift(v, stage, d) for d in (1, 2, 3)])


def ring_gather(v):
    before, after = torus_shift(v, 1, 1), torus_shift(v, 1, -1)
    return v, before, after, torus_shift(before[:2], 1, 1), torus_shift(after[2:], 1, -1)


def first_exchange(x0, x1, x2):
    return other_chip(x0), x1, other_core(x2)


def second_exchange(left, own, right):
    up = far_band(jnp.stack([left[0], own[0], right[0]]))
    down = near_band(jnp.stack([left[2], own[2], right[2]]))
    return up, down


def body(grid_latent, mesh_latent, w_src_enc, w_dst_enc, w_out_enc, w_src_dec, w_dst_dec, w_out_dec, grid_cot,
         enc_send, enc_slot, enc_count, dec_send, dec_slot, dec_count):
    core, _, _, z = place()
    odd = z & 1
    sends = jnp.concatenate([enc_send, dec_send], axis=0)
    sends = jnp.where(odd == 1, sends[:, ::-1], sends)
    sends = jnp.where(core == 1, sends[:, :, ::-1], sends)
    sends = jnp.pad(sends.reshape(2, 9, CAP), ((0, 0), (0, 7), (0, 0))).reshape(32, CAP)

    block = ((3, ROWS, D), BF)
    one = ((ROWS, D), BF)
    x0, own0, own1, own2, x2 = call(pick_rows, [block, one, one, one, block], "pick_rows", 1300000000)(sends, grid_latent)
    hot_enc, back_enc, target, upstream = call(
        prepare,
        [((KE * MD, 9 * CAP), BF), ((9 * CAP, KE * MD), BF), ((GD, D), F32), ((GD, D), F32)],
        "prepare", 4000000000,
    )(enc_slot.T, grid_latent, grid_cot, w_dst_dec, w_out_dec)
    down = near_band(own2)
    up = far_band(own0)
    left, right = other_chip(x0), other_core(x2)
    down2 = near_band(jnp.stack([left[2], right[2]]))
    up2 = far_band(jnp.stack([left[0], right[0]]))
    mean_enc, slope, mesh_new, table, recv = call(
        enc_forward,
        [((MD, D), BF), ((KE, MD, D), BF), ((MD, D), BF), ((16, CAP), F32), ((9 * CAP, D), BF)],
        "enc_forward", 3400000000, scratch=[pltpu.VMEM((9 * CAP, D), BF)],
    )(up, up2, down, down2, left, right, own1, hot_enc, enc_count.reshape(1, MD), mesh_latent, w_src_enc, w_dst_enc, w_out_enc)

    up = far_band(mesh_new)
    down = near_band(mesh_new)
    hot_dec, back_dec = call(
        merge_index, [((4, KD * STEP, NEAR), BF), ((4, 9 * MD, KD * STEP), BF)], "merge_index", 2000000000
    )(table, dec_slot.T)
    up, down, hot_dec, back_dec = lax.optimization_barrier((up, down, hot_dec, back_dec))
    mine = jnp.stack([up, mesh_new, down])
    left = other_chip(mine)
    right = other_core(mine)
    near = [jnp.concatenate([left[a], mine[a], right[a]], axis=0) for a in range(3)]

    rows = ((GD, D), BF)
    mean_dec, dst_dec, slots_dec, b0, b1, b2 = call(
        decoder,
        [rows, rows, ((9 * MD, D), BF)] + [((3, MD, D), BF)] * 3,
        "decoder", 5500000000,
        scratch=[pltpu.VMEM((NEAR, D), BF), pltpu.VMEM((9 * MD, D), F32)],
    )(*near, hot_dec, back_dec, dec_count.reshape(1, GD), target, upstream, w_src_dec)

    left = other_chip(b0)
    right = other_core(b2)
    sums = [left[a].astype(F32) + b1[a].astype(F32) + right[a].astype(F32) for a in range(3)]
    up = far_band(sums[0].astype(BF))
    down = near_band(sums[2].astype(BF))

    half = ((4, 4, 3, 16, D), BF)
    *packed_dec, grid_part = call(
        dec_grads, [half, half, ((GD, D), F32)], "dec_grads", 2300000000, scratch=[pltpu.VMEM((3, D, D), F32)],
    )(*near, slots_dec, grid_latent, dst_dec, mean_dec, grid_cot, w_dst_dec)

    mesh_grad, dround, dst_enc, slots_enc, x0, x1, x2 = call(
        enc_backward,
        [((MD, D), F32), ((MD, D), BF), ((MD, D), BF), ((9 * CAP, D), BF)] + [((3, CAP, D), BF)] * 3,
        "enc_backward", 3200000000, scratch=[pltpu.VMEM((KE * MD, D), BF)],
    )(up, sums[1], down, slope, back_enc, w_src_enc, w_dst_enc, w_out_enc)
    packed_enc = call(
        enc_grads, [half, half], "enc_grads", 700000000, scratch=[pltpu.VMEM((3, D, D), F32)],
    )(recv, slots_enc, mesh_latent, dst_enc, mean_enc, dround)

    left, _, right = first_exchange(x0, x1, x2)
    enc, dec = chip_sum(packed_enc, packed_dec)
    on, back = first_step(enc, dec)
    on, back, left, right = lax.optimization_barrier((on, back, left, right))
    up, down = second_exchange(left, x1, right)
    part_sums = first_sum(enc, dec, on, back)
    part_sum = second_sum(part_sums)
    (grid_grad,) = call(put_rows, [((GD, D), F32)], "put_rows", 1300000000)(
        sends, up, left, x1, right, down, grid_part
    )
    v = gather(stage_three(part_sum), 2)
    v, grid_grad = lax.optimization_barrier((v, grid_grad))
    parts = ring_gather(v)
    others = [other_core(part) for part in parts]
    square = ((D, D), F32)
    anywhere = pl.BlockSpec(memory_space=pl.ANY)
    unpacker = functools.partial(
        call, outs=[square] * 6, flops=50000000,
        scratch=[pltpu.VMEM((6, 256, D), F32), pltpu.SemaphoreType.DMA((6,))], out_specs=[anywhere] * 6,
    )
    grads = unpacker(functools.partial(unpack, 0), name="unpack_own")(*parts)
    grads = unpacker(
        functools.partial(unpack, 1), name="unpack_other",
        in_specs=[pl.BlockSpec(memory_space=pltpu.VMEM)] * 5 + [anywhere] * 6,
        input_output_aliases={m + 5: m for m in range(6)},
    )(*others, *grads)
    return (grid_grad, mesh_grad, *grads)


def solution(mesh):
    rows = P(AXES, None)
    whole = P()
    return jax.shard_map(
        body,
        mesh=mesh,
        in_specs=(rows, rows) + (whole,) * 6 + (rows, P(AXES, None, None, None), rows, P(AXES),
                                               P(AXES, None, None, None), rows, P(AXES)),
        out_specs=(rows, rows) + (whole,) * 6,
        check_vma=False,
    )
```
